512 devices in a mesh: dom: 64 (over y_hi, z, core), epoch: 8 (over x, y_lo).
Axes of the slice: x: 4, y: 4 (y_hi: 2, y_lo: 2; y = y_hi * 2 + y_lo), z: 16, core: 2. Of those that a mesh axis runs over, the one named last changes fastest.
Arguments:
- memory: bfloat16 [8, 32768, 256], P('epoch', 'dom'), may hold values from -6 to 6
- neighbours: int32 [32768, 10], P('dom'), may hold values from 0 to 511
- owners: int32 [8, 8192, 2], P('epoch', 'dom'), may hold values from 0 to 63, all different within a row; in each aligned block of 128 rows (0 to 127, 128 to 255, ..., all dimensions but the last counted through in order) at most 8 rows name the same one
- rows: int32 [8, 8192, 2], P('epoch', 'dom'), may hold values from 0 to 511
- edge_feat: bfloat16 [8, 8192, 128], P('epoch', 'dom'), may hold values from -24 to 24
- labels: int32 [8, 8192], P('epoch', 'dom'), may hold values 0 or 1
- w_query: bfloat16 [256, 256], replicated, may hold values from -0.375 to 0.375
- w_keyval: bfloat16 [256, 512], replicated, may hold values from -0.375 to 0.375
- w_out: bfloat16 [256, 256], replicated, may hold values from -0.375 to 0.375
- w_msg_mem: bfloat16 [256, 256], replicated, may hold values from -0.375 to 0.375
- w_msg_edge: bfloat16 [128, 256], replicated, may hold values from -0.5 to 0.5
- w_pair_edge: bfloat16 [128, 256], replicated, may hold values from -0.5 to 0.5
- gru_input: bfloat16 [256, 768], replicated, may hold values from -0.375 to 0.375
- gru_hidden: bfloat16 [256, 768], replicated, may hold values from -0.375 to 0.375
- gru_bias: float32 [768], replicated, may hold values from -0.5 to 0.5
- bn_gain: float32 [256], replicated, may hold values from 0.1 to 1.9
- bn_shift: float32 [256], replicated, may hold values from -3 to 3
- w_score: bfloat16 [256], replicated, may hold values from -1 to 1
Outputs:
- new_memory: bfloat16 [8, 32768, 256], P('epoch', 'dom')
- loss: float32 [8], P('epoch')
The draws below stay inside these ranges and needn't reach their ends.
Inputs may be any that keep to these rules, and one draw needn't show every extreme that they name: Within the 128 events of one device, no partition owns more than 8 endpoints, and some partition owns exactly 8; an event's two endpoints have different owners.
All inputs are finite; a program needn't handle non-finite values. No bound on the sum of `labels` on one device may be relied on, other than what follows from the above.
Results may differ from the reference program's by a relative error of at most 0.001.
The reference program's roundings to bfloat16 on the way count: a program that leaves them out, or rounds other values in their place, can miss the bound.
Values may be sent and summed in bfloat16 or wider, within the bound.
A program may use at most 64 MiB of HBM per device.

```python
import math
import jax
import jax.numpy as jnp
import numpy as np
from jax import lax

W = 256
EF = 128
HEADS = 2
NBR = 10
NODE_DEV = 512
EV_DEV = 128
HD = 128
CAP = 8
NODES = 32768
EVENTS = 8192
N_DOM = 64
N_EPOCH = 8


def draw_edge_feat(key, part):
    key = jax.random.fold_in(key, 7)
    first = jax.random.fold_in(key, 0)
    rising = 1.0 + 2.0 * jnp.arange(EVENTS, dtype=jnp.float32) / EVENTS
    base = jnp.clip(jax.random.normal(first, (N_EPOCH, EVENTS, EF), jnp.float32), -6.0, 6.0)
    vals = base * rising[None, :, None]
    return vals.astype(jnp.bfloat16)


def plant(array, rng, least, largest):
    shape = array.shape
    index_at = [jax.random.randint(jax.random.fold_in(rng, axis), (), 0, shape[axis]) for axis in range(len(shape))]
    array = array.at[tuple(index_at)].set(least)
    longest = shape.index(max(shape))
    index_at[longest] = (index_at[longest] + 1) % shape[longest]
    return array.at[tuple(index_at)].set(largest)


def block_scale(key, dims, shards, least, largest):
    def one(dim, shards_of):
        draws = jax.random.uniform(jax.random.fold_in(jax.random.fold_in(key, 6), dim), (shards_of,), jnp.float32, least / len(shards), largest / len(shards))
        return jnp.repeat(jnp.exp(draws), dims[dim] // shards_of).reshape((-1,) + (1,) * (len(dims) - dim - 1))

    loudness = one(*shards[0])
    for cut in shards[1:]:
        loudness = loudness * one(*cut)
    return loudness


def routed_block(key, own, number, rows, number_of, top, most, lean):
    order = jax.random.permutation(key, number_of)
    heavy_load, usual = shares(number_of, rows * top, most, lean, True), shares(number_of, rows * top, most, lean, False)
    places = jnp.arange(number_of)

    def named(sizes, offset_by):
        used = int((sizes > 0).sum())
        fixed = max(1, used // 4)
        shifted = fixed + (places - fixed + offset_by * (used - fixed)) % max(1, number_of - fixed)
        return jnp.zeros((number_of,), jnp.int32).at[order[jnp.where(places < fixed, places, shifted)]].set(jnp.asarray(sizes, jnp.int32))

    sizes = jnp.where(number % 4 == 0, named(heavy_load, number // 4), named(usual, number - number // 4 - 1))
    mixed = jax.random.permutation(jax.random.fold_in(own, 3), number_of)
    source_of, taker = mixed[0:number_of // 2 * 2:2], mixed[1:number_of // 2 * 2:2]
    slack = jnp.minimum(sizes[source_of] - 1, most - sizes[taker]) // 2
    slack = jnp.where((source_of == order[0]) | (taker == order[0]) | (sizes[taker] == 0), 0, jnp.maximum(slack, 0))
    shifted = jax.random.randint(jax.random.fold_in(own, 4), (number_of // 2,), 0, 1 << 20) % (slack + 1)
    sizes = sizes.at[source_of].add(-shifted).at[taker].add(shifted)
    items = jnp.searchsorted(jnp.cumsum(sizes), jnp.arange(rows * top), side="right").astype(jnp.int32)
    listing = items.reshape(top, rows).T
    listing = listing[jax.random.permutation(jax.random.fold_in(own, 1), rows)]
    offset_by = jax.random.randint(jax.random.fold_in(own, 2), (rows, 1), 0, top)
    return jnp.take_along_axis(listing, (jnp.arange(top)[None, :] + offset_by) % top, axis=1)


def shares(amount, total, limit, lean, full):
    loads = [(1 << 20) // math.isqrt(grade ** lean) + 1 for grade in range(1, amount + 1)]
    largest = limit if full else min(limit, max(-(-total // amount), total * loads[0] // sum(loads)))
    least = 1 if total - largest >= amount - 1 else 0
    given, surplus = [largest] + [least] * (amount - 1), total - largest - least * (amount - 1)
    while surplus > 0:
        free = [i for i in range(1, amount) if given[i] < largest] or [i for i in range(1, amount) if given[i] < limit]
        whole, remaining = sum([loads[i] for i in free]), surplus
        for i in free:
            addition = min(limit - given[i], max(1, remaining * loads[i] // whole), surplus)
            given[i] = given[i] + addition
            surplus = surplus - addition
    return np.array(given)


def scatter_about(rng, shape, deviation, limit, cuts=(), kind=jnp.bfloat16):
    entries = deviation * jax.random.normal(rng, shape, jnp.float32)
    if cuts:
        entries = entries * block_scale(rng, shape, cuts, -0.22, 0.18)
    return jnp.clip(entries, -limit, limit).astype(kind)


def setup_inputs(seed: int = 0) -> dict:
    arg_keys = jax.random.split(jax.random.key(seed), 19)
    memory = scatter_about(arg_keys[0], (N_EPOCH, NODES, W), 1.0, 6.0, ((0, 8), (1, 64)))
    neighbours = plant(jax.random.randint(arg_keys[1], (NODES, NBR), 0, NODE_DEV), jax.random.fold_in(arg_keys[1], 1), 0, NODE_DEV - 1).astype(jnp.int32)
    owners_keys = jax.random.split(jax.random.fold_in(arg_keys[2], 1), N_EPOCH * EVENTS // EV_DEV)
    owners_turns = jax.random.permutation(jax.random.fold_in(arg_keys[2], 3), N_EPOCH * EVENTS // EV_DEV)
    owners = jax.vmap(lambda own, number: routed_block(jax.random.fold_in(arg_keys[2], 2), own, number, EV_DEV, N_DOM, 2, CAP, 2))(owners_keys, owners_turns).reshape((N_EPOCH, EVENTS, 2))
    rows = plant(jax.random.randint(arg_keys[3], (N_EPOCH, EVENTS, 2), 0, NODE_DEV), jax.random.fold_in(arg_keys[3], 1), 0, NODE_DEV - 1).astype(jnp.int32)
    edge_feat = draw_edge_feat(jax.random.fold_in(arg_keys[18], 71), 0)
    labels = plant((jax.random.randint(arg_keys[5], (N_EPOCH, EVENTS), 0, 2) < 1).astype(jnp.int32), jax.random.fold_in(arg_keys[5], 1), 0, 1)
    w_query = scatter_about(arg_keys[6], (W, W), W ** -0.5, 0.375)
    w_keyval = scatter_about(arg_keys[7], (W, 2 * W), W ** -0.5, 0.375)
    w_out = scatter_about(arg_keys[8], (W, W), W ** -0.5, 0.375)
    w_msg_mem = scatter_about(arg_keys[9], (W, W), W ** -0.5, 0.375)
    w_msg_edge = scatter_about(arg_keys[10], (EF, W), EF ** -0.5, 0.5)
    w_pair_edge = scatter_about(arg_keys[11], (EF, W), EF ** -0.5, 0.5)
    gru_input = scatter_about(arg_keys[12], (W, 3 * W), W ** -0.5, 0.375)
    gru_hidden = scatter_about(arg_keys[13], (W, 3 * W), W ** -0.5, 0.375)
    gru_bias = jnp.clip(jax.random.uniform(arg_keys[14], (3 * W,), jnp.float32, -0.5, 0.5), -0.5, 0.5)
    bn_gain = jnp.clip(1.0 + 0.18 * jax.random.normal(arg_keys[15], (W,), jnp.float32), 0.1, 1.9)
    bn_shift = scatter_about(arg_keys[16], (W,), 0.5, 3.0, (), jnp.float32)
    w_score = scatter_about(arg_keys[17], (W,), (W // 9) ** -0.5, 1.0)
    return dict(memory=memory, neighbours=neighbours, owners=owners, rows=rows, edge_feat=edge_feat, labels=labels, w_query=w_query, w_keyval=w_keyval, w_out=w_out, w_msg_mem=w_msg_mem, w_msg_edge=w_msg_edge, w_pair_edge=w_pair_edge, gru_input=gru_input, gru_hidden=gru_hidden, gru_bias=gru_bias, bn_gain=bn_gain, bn_shift=bn_shift, w_score=w_score)


def group_step(mem, neighbours, own, loc, feat, lab, w_query, w_keyval, w_out, w_msg_mem, w_msg_edge, w_pair_edge, gru_input, gru_hidden, gru_bias, bn_gain, bn_shift, w_score):
    width = mem.shape[1]
    gid = (own * NODE_DEV + loc).astype(jnp.int32)
    flat = gid.reshape(-1)
    mrow = mem[flat]
    query = jnp.dot(mrow, w_query, preferred_element_type=jnp.float32).astype(jnp.bfloat16)
    nbr_ids = ((flat // NODE_DEV)[:, None] * NODE_DEV + neighbours[flat]).astype(jnp.int32)
    keyval = jnp.dot(mem[nbr_ids], w_keyval, preferred_element_type=jnp.float32).astype(jnp.bfloat16)
    count_p = flat.shape[0]
    keys = keyval[:, :, :width].reshape(count_p, NBR, HEADS, HD).astype(jnp.float32)
    values = keyval[:, :, width:].reshape(count_p, NBR, HEADS, HD).astype(jnp.float32)
    qh = query.reshape(count_p, HEADS, HD).astype(jnp.float32)
    scores = jnp.einsum('phd,pjhd->phj', qh, keys) / jnp.sqrt(jnp.float32(HD))
    probs = jax.nn.softmax(scores, axis=-1).astype(jnp.bfloat16)
    attended = jnp.einsum('phj,pjhd->phd', probs.astype(jnp.float32), values).astype(jnp.bfloat16).reshape(count_p, width)
    embed = (mrow.astype(jnp.float32) + jnp.dot(attended, w_out, preferred_element_type=jnp.float32)).astype(jnp.bfloat16)
    embed = embed.reshape(-1, 2, width)
    pair = embed[:, 0].astype(jnp.float32) * embed[:, 1].astype(jnp.float32) + jnp.dot(feat, w_pair_edge, preferred_element_type=jnp.float32)
    total = jnp.float32(pair.shape[0])
    mean = lax.optimization_barrier(jnp.sum(pair, axis=0)) / total
    var = lax.optimization_barrier(jnp.sum(pair * pair, axis=0)) / total - mean * mean
    normed = (pair - mean) * lax.rsqrt(var + 1e-05) * bn_gain + bn_shift
    logit = jnp.dot(jax.nn.relu(normed), w_score.astype(jnp.float32), precision=lax.Precision.HIGHEST)
    loss = jnp.sum(jax.nn.softplus(logit) - lab.astype(jnp.float32) * logit) / total
    mrow3 = mrow.reshape(-1, 2, width)
    other = mrow3[:, ::-1]
    message = (jnp.dot(other, w_msg_mem, preferred_element_type=jnp.float32) + jnp.dot(feat, w_msg_edge, preferred_element_type=jnp.float32)[:, None, :]).astype(jnp.bfloat16).reshape(-1, width)
    agg = jax.ops.segment_sum(message.astype(jnp.float32), flat, num_segments=mem.shape[0])
    count = jax.ops.segment_sum(jnp.ones(flat.shape, jnp.float32), flat, num_segments=mem.shape[0])
    avg = (agg[flat] / jnp.maximum(count[flat], 1.0)[:, None]).astype(jnp.bfloat16)
    fresh = gru(avg, mrow, gru_input, gru_hidden, gru_bias)
    updated = mem.at[flat].set(fresh)
    touched = jnp.zeros((mem.shape[0],), jnp.float32).at[flat].set(1.0)
    return (updated, touched, loss)

def gru(avg, hidden, gru_input, gru_hidden, gru_bias):
    width = hidden.shape[1]
    inp = jnp.dot(avg, gru_input, preferred_element_type=jnp.float32) + gru_bias
    hid = jnp.dot(hidden, gru_hidden, preferred_element_type=jnp.float32)
    reset = jax.nn.sigmoid(inp[:, :width] + hid[:, :width])
    update = jax.nn.sigmoid(inp[:, width:2 * width] + hid[:, width:2 * width])
    cand = jnp.tanh(inp[:, 2 * width:] + reset * hid[:, 2 * width:])
    return ((1.0 - update) * cand + update * hidden.astype(jnp.float32)).astype(jnp.bfloat16)

def reference(memory, neighbours, owners, rows, edge_feat, labels, w_query, w_keyval, w_out, w_msg_mem, w_msg_edge, w_pair_edge, gru_input, gru_hidden, gru_bias, bn_gain, bn_shift, w_score):
    outputs = []
    losses = []
    prev_updated = memory[0]
    prev_touched = jnp.zeros((memory.shape[1],), jnp.float32)
    for group in range(N_EPOCH):
        mem = memory[group]
        updated, touched, loss = group_step(mem, neighbours, owners[group], rows[group], edge_feat[group], labels[group], w_query, w_keyval, w_out, w_msg_mem, w_msg_edge, w_pair_edge, gru_input, gru_hidden, gru_bias, bn_gain, bn_shift, w_score)
        prior = jnp.where(prev_touched[:, None] > 0, prev_updated, mem)
        outputs.append(jnp.where(touched[:, None] > 0, updated, prior))
        losses.append(loss)
        prev_updated = updated
        prev_touched = touched
    return (jnp.stack(outputs), jnp.stack(losses))
```

```python
import functools

import jax
import jax.numpy as jnp
from jax import lax
from jax.experimental import pallas as pl
from jax.experimental.pallas import tpu as pltpu
from jax.sharding import PartitionSpec as P

MESH = pl.DeviceIdType.MESH
F32 = jnp.float32
BF16 = jnp.bfloat16
CAP = 8
HEADS = 2
LANES = 128
CORES = 2
HALVES = 2
PLANE = CORES * HALVES
UNTOUCHED = 1e30
NODE_CHUNKS = 4


def iota(shape, dim):
    return lax.broadcasted_iota(jnp.int32, shape, dim)


def dot(a, b):
    return jnp.dot(a, b, preferred_element_type=F32)


def dot_nt(a, b):
    return lax.dot_general(a, b, (((1,), (1,)), ((), ())), preferred_element_type=F32)


def dot_tn(a, b):
    return lax.dot_general(a, b, (((0,), (0,)), ((), ())), preferred_element_type=F32)


def onehot(mask):
    return jnp.where(mask, 1.0, 0.0).astype(BF16)


def pack(x):
    rows = x.shape[0] // CAP
    left = x[:, :LANES].reshape(rows, CAP, LANES)
    right = x[:, LANES:].reshape(rows, CAP, LANES)
    return jnp.concatenate([left, right], axis=1).astype(BF16)


def unpack(x):
    rows = x.shape[0]
    x = x.astype(F32)
    left = x[:, :CAP].reshape(rows * CAP, LANES)
    right = x[:, CAP:].reshape(rows * CAP, LANES)
    return jnp.concatenate([left, right], axis=1).astype(BF16)


def peer_at(me, step, parts):
    rings = parts // PLANE
    step = step + jnp.where(step >= parts - PLANE, 1, 0)
    turn, inside = step // PLANE, step % PLANE
    half = (turn + 1) // 2
    along = rings // 2 + jnp.where(turn % 2 == 1, half, rings - half)
    y, rest = me // (rings * CORES), me % (rings * CORES)
    z, core = rest // CORES, rest % CORES
    spot = (y * CORES + core + inside) % PLANE
    return (spot // CORES) * (rings * CORES) + ((z + along) % rings) * CORES + spot % CORES


def plane_peer(me, by, parts):
    rings = parts // PLANE
    y, rest = me // (rings * CORES), me % (rings * CORES)
    z, core = rest // CORES, rest % CORES
    spot = (y * CORES + core + by) % PLANE
    return (spot // CORES) * (rings * CORES) + z * CORES + spot % CORES


def kernel(
    parts,
    groups,
    table,
    nbr,
    own,
    row,
    feat,
    lab,
    w_query,
    w_keyval,
    w_out,
    w_msg_mem,
    w_msg_edge,
    w_pair_edge,
    gru_input,
    gru_hidden,
    gru_bias,
    bn_gain,
    bn_shift,
    w_score,
    out,
    loss,
    req_s,
    req_r,
    mem_s,
    mem_r,
    emb_s,
    emb_r,
    msg_s,
    msg_r,
    st_s,
    st_r,
    tot_s,
    tot_r,
    ls_s,
    ls_r,
    hand_s,
    hand_r,
    keyval,
    query,
    attended,
    embed,
    hidden,
    pick,
    pick_t,
    place_s,
    place_t,
    send_sem,
    recv_sem,
    st_send,
    st_recv,
    hand_send,
    hand_recv,
):
    me = lax.axis_index("dom")
    group = lax.axis_index("epoch")
    after = lax.rem(group + 1, groups)
    ahead = lax.rem(group + groups - 1, groups)
    nodes, width = table.shape
    events = feat.shape[0]
    slots = parts * CAP
    hsize = width // HEADS

    barrier = pltpu.get_barrier_semaphore()

    def greet(step, carry):
        pl.semaphore_signal(
            barrier, inc=1, device_id={"dom": peer_at(me, step, parts)}, device_id_type=MESH
        )
        return carry

    lax.fori_loop(0, parts - 1, greet, 0)
    pl.semaphore_signal(barrier, inc=1, device_id={"epoch": ahead}, device_id_type=MESH)

    def send_all(src, dst, which):
        def one(step, carry):
            peer = peer_at(me, step, parts)
            pltpu.make_async_remote_copy(
                src_ref=src(peer),
                dst_ref=dst.at[me],
                send_sem=send_sem.at[which],
                recv_sem=recv_sem.at[which],
                device_id={"dom": peer},
                device_id_type=MESH,
            ).start()
            return carry

        lax.fori_loop(0, parts - 1, one, 0)
        pltpu.make_async_copy(src(me), dst.at[me], recv_sem.at[which]).start()

    def wait_recv(dst, which):
        pltpu.make_async_copy(dst, dst, recv_sem.at[which]).wait()

    def wait_send(dst, which):
        sent = dst.at[pl.ds(0, parts - 1)]
        pltpu.make_async_copy(sent, sent, send_sem.at[which]).wait()

    ends = 2 * events
    o = jnp.concatenate([own[0:1, :], own[1:2, :]], axis=1)
    r = jnp.concatenate([row[0:1, :], row[1:2, :]], axis=1) + 1
    owned = iota((parts, ends), 0) == o
    owned_b = onehot(owned)
    earlier = onehot(iota((ends, ends), 0) < iota((ends, ends), 1))
    before = dot(owned_b, earlier)
    rank = jnp.sum(jnp.where(owned, before, 0.0), axis=0, keepdims=True)
    rank_i = rank.astype(jnp.int32)
    ranked = iota((LANES, ends), 0) == rank_i
    high = jnp.where(ranked, (r // 32).astype(F32), 0.0).astype(BF16)
    low = jnp.where(ranked, (r % 32).astype(F32), 0.0).astype(BF16)
    asked = dot_nt(owned_b, high) * 32.0 + dot_nt(owned_b, low)
    req_s[...] = asked.reshape(parts, 1, LANES)

    pl.semaphore_wait(barrier, parts)
    send_all(lambda peer: req_s.at[peer], req_r, 0)

    place = o * CAP + rank_i
    place_s[...] = onehot(iota((slots, ends), 0) == place)
    diagonal = iota((ends, ends), 0) == iota((ends, ends), 1)
    place_col = jnp.sum(jnp.where(diagonal, place.astype(F32), 0.0), axis=1, keepdims=True)
    place_t[...] = onehot(iota((ends, slots), 1) == place_col.astype(jnp.int32))

    keyval[...] = dot(table[...], w_keyval[...]).astype(BF16)
    query[...] = dot(table[...], w_query[...]).astype(BF16)
    block = LANES
    scale = 1.0 / jnp.sqrt(jnp.float32(hsize))
    for b in range(nodes // block):
        here = pl.ds(b * block, block)
        times = jnp.zeros((nodes, block), F32)
        for j in range(nbr.shape[0]):
            times = times + jnp.where(iota((nodes, block), 0) == nbr[j : j + 1, here], 1.0, 0.0)
        for h in range(HEADS):
            cols = pl.ds(h * hsize, hsize)
            score = dot_nt(keyval[:, cols], query[here, cols]) * scale
            score = jnp.where(times > 0, score, -1e30)
            top = jnp.max(score, axis=0, keepdims=True)
            grown = jnp.exp(score - top)
            total = jnp.sum(grown * times, axis=0, keepdims=True)
            weight = (grown / total).astype(BF16).astype(F32) * times
            main = weight.astype(BF16)
            rest = (weight - main.astype(F32)).astype(BF16)
            value = keyval[:, pl.ds(width + h * hsize, hsize)]
            attended[here, cols] = (dot_tn(main, value) + dot_tn(rest, value)).astype(BF16)
    embed[...] = (table[...].astype(F32) + dot(attended[...], w_out[...])).astype(BF16)

    wait_recv(req_r, 0)
    got = jnp.broadcast_to(req_r[...], (parts, CAP, LANES))
    mine = iota((parts, CAP, LANES), 1) == iota((parts, CAP, LANES), 2)
    wanted = jnp.sum(jnp.where(mine, got, 0.0), axis=2, keepdims=True).reshape(slots, 1)
    wanted = wanted.astype(jnp.int32)
    pick[...] = onehot(iota((slots, nodes), 1) + 1 == wanted)
    mem_s[...] = pack(dot(pick[...], table[...]))
    send_all(lambda peer: mem_s.at[peer], mem_r, 1)
    emb_s[...] = pack(dot(pick[...], embed[...]))
    send_all(lambda peer: emb_s.at[peer], emb_r, 2)

    square = iota((slots, slots), 0) == iota((slots, slots), 1)
    wanted_row = jnp.sum(jnp.where(square, wanted.astype(F32), 0.0), axis=0, keepdims=True)
    pick_t[...] = onehot(iota((nodes, slots), 0) + 1 == wanted_row.astype(jnp.int32))
    hidden[...] = dot(table[...], gru_hidden[...])
    msg_edge = dot(feat[...], w_msg_edge[...])
    pair_edge = dot(feat[...], w_pair_edge[...])

    wait_recv(mem_r, 1)
    rows_back = dot(place_t[...], unpack(mem_r[...])).astype(BF16)
    to_src = dot(rows_back[events:], w_msg_mem[...]) + msg_edge
    to_dst = dot(rows_back[:events], w_msg_mem[...]) + msg_edge
    message = jnp.concatenate([to_src, to_dst], axis=0).astype(BF16)
    msg_s[...] = pack(dot(place_s[...], message))
    send_all(lambda peer: msg_s.at[peer], msg_r, 3)

    wait_recv(emb_r, 2)
    ends_back = dot(place_t[...], unpack(emb_r[...]))
    pair = ends_back[:events] * ends_back[events:] + pair_edge
    sum_one = jnp.sum(pair, axis=0, keepdims=True)
    sum_two = jnp.sum(pair * pair, axis=0, keepdims=True)
    quarters = [
        sum_one[:, :LANES],
        sum_one[:, LANES:],
        sum_two[:, :LANES],
        sum_two[:, LANES:],
    ]
    for k, quarter in enumerate(quarters):
        st_s[k] = quarter
    copies = []
    for by in range(1, PLANE):
        copies.append(
            pltpu.make_async_remote_copy(
                src_ref=st_s,
                dst_ref=st_r.at[by - 1],
                send_sem=st_send.at[by - 1],
                recv_sem=st_recv.at[by - 1],
                device_id={"dom": plane_peer(me, by, parts)},
                device_id_type=MESH,
            )
        )
    for copy in copies:
        copy.start()
    for copy in copies:
        copy.wait()
    tot_s[...] = st_s[...] + st_r[0] + st_r[1] + st_r[2]
    rings = parts // PLANE
    spot = (me // (rings * CORES)) * CORES + me % CORES
    send_all(lambda peer: tot_s.at[spot], tot_r, 4)

    wait_recv(msg_r, 3)
    inbox = unpack(msg_r[...])
    chunk = nodes // NODE_CHUNKS
    hands = []
    for c in range(NODE_CHUNKS):
        here = pl.ds(c * chunk, chunk)
        picked = pick_t[here, :]
        count = jnp.sum(picked.astype(F32), axis=1, keepdims=True)
        avg = (dot(picked, inbox) / jnp.maximum(count, 1.0)).astype(BF16)
        inp = dot(avg, gru_input[...]) + gru_bias[...]
        hid = hidden[here, :]
        reset = jax.nn.sigmoid(inp[:, :width] + hid[:, :width])
        update = jax.nn.sigmoid(inp[:, width : 2 * width] + hid[:, width : 2 * width])
        cand = jnp.tanh(inp[:, 2 * width :] + reset * hid[:, 2 * width :])
        fresh = (1.0 - update) * cand + update * table[here, :].astype(F32)
        hand_s[here, :] = jnp.where(count > 0, fresh, UNTOUCHED).astype(BF16)
        hand = pltpu.make_async_remote_copy(
            src_ref=hand_s.at[here],
            dst_ref=hand_r.at[here],
            send_sem=hand_send.at[c],
            recv_sem=hand_recv.at[c],
            device_id={"epoch": after},
            device_id_type=MESH,
        )
        hand.start()
        hands.append(hand)

    wait_recv(tot_r, 4)
    sums = [jnp.zeros((1, LANES), F32) for _ in range(PLANE)]
    for k in range(PLANE):
        for z in range(rings):
            sums[k] = sums[k] + tot_r[(k // CORES) * rings * CORES + z * CORES + k % CORES]
    count_all = jnp.float32(events * parts)
    mean = jnp.concatenate([sums[0], sums[1]], axis=1) / count_all
    var = jnp.concatenate([sums[2], sums[3]], axis=1) / count_all - mean * mean
    normed = (pair - mean) * lax.rsqrt(var + 1e-05) * bn_gain[...] + bn_shift[...]
    weighed = jnp.maximum(normed, 0.0) * w_score[...].astype(F32)
    logit_col = jnp.sum(weighed, axis=1, keepdims=True)
    corner = iota((events, events), 0) == iota((events, events), 1)
    logit = jnp.sum(jnp.where(corner, logit_col, 0.0), axis=0, keepdims=True)
    soft = jnp.maximum(logit, 0.0) + jnp.log1p(jnp.exp(-jnp.abs(logit)))
    terms = soft - lab[...].astype(F32) * logit
    ls_s[...] = jnp.broadcast_to(jnp.sum(terms, axis=1, keepdims=True), (1, LANES))
    send_all(lambda peer: ls_s, ls_r, 5)

    for c in range(NODE_CHUNKS):
        here = pl.ds(c * chunk, chunk)
        hands[c].wait()
        handed = hand_r[here, :].astype(F32)
        fresh = hand_s[here, :].astype(F32)
        old = table[here, :].astype(F32)
        prior = jnp.where(jnp.logical_and(handed < UNTOUCHED / 2, group > 0), handed, old)
        out[here, :] = jnp.where(fresh < UNTOUCHED / 2, fresh, prior).astype(BF16)

    wait_recv(ls_r, 5)
    loss[...] = jnp.sum(ls_r[...], axis=0) / count_all

    wait_send(req_s, 0)
    wait_send(mem_s, 1)
    wait_send(emb_s, 2)
    wait_send(msg_s, 3)
    wait_send(tot_r, 4)
    wait_send(ls_r, 5)


def shards(
    parts,
    groups,
    memory,
    neighbours,
    owners,
    rows,
    edge_feat,
    labels,
    w_query,
    w_keyval,
    w_out,
    w_msg_mem,
    w_msg_edge,
    w_pair_edge,
    gru_input,
    gru_hidden,
    gru_bias,
    bn_gain,
    bn_shift,
    w_score,
):
    nodes, width = memory.shape[1:]
    events = owners.shape[1]
    slots = parts * CAP
    ends = 2 * events
    block = (parts, 2 * CAP, LANES)
    line = (parts, 1, LANES)
    result, loss = pl.pallas_call(
        functools.partial(kernel, parts, groups),
        out_shape=(
            jax.ShapeDtypeStruct((nodes, width), BF16),
            jax.ShapeDtypeStruct((1, LANES), F32),
        ),
        in_specs=[pl.BlockSpec(memory_space=pltpu.VMEM)] * 18,
        out_specs=(pl.BlockSpec(memory_space=pltpu.VMEM),) * 2,
        scratch_shapes=[
            pltpu.VMEM(line, F32),
            pltpu.VMEM(line, F32),
            pltpu.VMEM(block, BF16),
            pltpu.VMEM(block, BF16),
            pltpu.VMEM(block, BF16),
            pltpu.VMEM(block, BF16),
            pltpu.VMEM(block, BF16),
            pltpu.VMEM(block, BF16),
            pltpu.VMEM((PLANE, 1, LANES), F32),
            pltpu.VMEM((PLANE - 1, PLANE, 1, LANES), F32),
            pltpu.VMEM((PLANE, 1, LANES), F32),
            pltpu.VMEM(line, F32),
            pltpu.VMEM((1, LANES), F32),
            pltpu.VMEM(line, F32),
            pltpu.VMEM((nodes, width), BF16),
            pltpu.VMEM((nodes, width), BF16),
            pltpu.VMEM((nodes, 2 * width), BF16),
            pltpu.VMEM((nodes, width), BF16),
            pltpu.VMEM((nodes, width), BF16),
            pltpu.VMEM((nodes, width), BF16),
            pltpu.VMEM((nodes, 3 * width), F32),
            pltpu.VMEM((slots, nodes), BF16),
            pltpu.VMEM((nodes, slots), BF16),
            pltpu.VMEM((slots, ends), BF16),
            pltpu.VMEM((ends, slots), BF16),
            pltpu.SemaphoreType.DMA((6,)),
            pltpu.SemaphoreType.DMA((6,)),
            pltpu.SemaphoreType.DMA((PLANE - 1,)),
            pltpu.SemaphoreType.DMA((PLANE - 1,)),
            pltpu.SemaphoreType.DMA((NODE_CHUNKS,)),
            pltpu.SemaphoreType.DMA((NODE_CHUNKS,)),
        ],
        compiler_params=pltpu.CompilerParams(
            collective_id=0, has_side_effects=True, vmem_limit_bytes=48 * 1024 * 1024
        ),
        name="window",
    )(
        memory[0],
        neighbours.T,
        owners[0].T,
        rows[0].T,
        edge_feat[0],
        labels,
        w_query,
        w_keyval,
        w_out,
        w_msg_mem,
        w_msg_edge,
        w_pair_edge,
        gru_input,
        gru_hidden,
        gru_bias[None],
        bn_gain[None],
        bn_shift[None],
        w_score[None],
    )
    return result[None], loss[0, :1]


def solution(mesh):
    parts, groups = mesh.shape["dom"], mesh.shape["epoch"]
    return jax.shard_map(
        functools.partial(shards, parts, groups),
        mesh=mesh,
        in_specs=(
            P("epoch", "dom", None),
            P("dom", None),
            P("epoch", "dom", None),
            P("epoch", "dom", None),
            P("epoch", "dom", None),
            P("epoch", "dom"),
            P(),
            P(),
            P(),
            P(),
            P(),
            P(),
            P(),
            P(),
            P(),
            P(),
            P(),
            P(),
        ),
        out_specs=(P("epoch", "dom", None), P("epoch")),
        check_vma=False,
    )
```

```python
import functools

import jax
import jax.numpy as jnp
from jax import lax
from jax.experimental import pallas as pl
from jax.experimental.pallas import tpu as pltpu
from jax.sharding import PartitionSpec as P

MESH = pl.DeviceIdType.MESH
F32 = jnp.float32
BF16 = jnp.bfloat16
VMEM_LIMIT = 62 * 1024 * 1024
CAP = 8
HEADS = 2
LANES = 128
CORES = 2
HALVES = 2
PLANE = CORES * HALVES
UNTOUCHED = 1e30
NODE_CHUNKS = 4
ORDER_M = (3, 2, 0, 1)
ORDER_E = (0, 1, 2, 3)
GROUPS = 4
TURNS = 4
EARLY = 3
LOAD_ORDER = (2, 3, 0, 7, 1, 6, 8, 4, 10, 9, 11, 13, 12, 14, 15, 16, 17, 5)


def iota(shape, dim):
    return lax.broadcasted_iota(jnp.int32, shape, dim)


def dot(a, b):
    return jnp.dot(a, b, preferred_element_type=F32)


def dot_nt(a, b):
    return lax.dot_general(a, b, (((1,), (1,)), ((), ())), preferred_element_type=F32)


def dot_tn(a, b):
    return lax.dot_general(a, b, (((0,), (0,)), ((), ())), preferred_element_type=F32)


def onehot(mask):
    return jnp.where(mask, 1.0, 0.0).astype(BF16)


def pack(x):
    rows = x.shape[0] // CAP
    left = x[:, :LANES].reshape(rows, CAP, LANES)
    right = x[:, LANES:].reshape(rows, CAP, LANES)
    return jnp.concatenate([left, right], axis=1).astype(BF16)


def unpack(x):
    rows = x.shape[0]
    x = x.astype(F32)
    left = x[:, :CAP].reshape(rows * CAP, LANES)
    right = x[:, CAP:].reshape(rows * CAP, LANES)
    return jnp.concatenate([left, right], axis=1).astype(BF16)


def along(turn, rings):
    half = (turn + 1) // 2
    if isinstance(turn, int):
        return rings // 2 + (half if turn % 2 else rings - half)
    return rings // 2 + jnp.where(lax.rem(turn, 2) == 1, half, rings - half)


def facing(turn, rings):
    if isinstance(turn, int):
        if turn in (0, rings - 1):
            return turn
        return turn + 1 if turn % 2 else turn - 1
    return turn + jnp.where(lax.rem(turn, 2) == 1, 1, -1)


def kernel(
    parts,
    groups,
    table_h,
    nbr_h,
    own_h,
    row_h,
    feat_h,
    lab_h,
    w_query_h,
    w_keyval_h,
    w_out_h,
    w_msg_mem_h,
    w_msg_edge_h,
    w_pair_edge_h,
    gru_input_h,
    gru_hidden_h,
    gru_bias_h,
    bn_gain_h,
    bn_shift_h,
    w_score_h,
    out,
    loss,
    req_s,
    req_r,
    mem_s,
    mem_r,
    emb_s,
    emb_r,
    msg_s,
    msg_r,
    st_r,
    tot_r,
    ls_r,
    hand_s,
    hand_r,
    keyval,
    query,
    attended,
    embed,
    hidden,
    pick,
    pick_t,
    place_s,
    place_t,
    times_named,
    agg,
    send_sem,
    recv_sem,
    tot_sem,
    ls_sem,
    st_send,
    st_recv,
    hand_send,
    hand_recv,
    load_sem,
    table,
    nbr,
    own,
    row,
    feat,
    lab,
    w_query,
    w_keyval,
    w_out,
    w_msg_mem,
    w_msg_edge,
    w_pair_edge,
    gru_input,
    gru_hidden,
    gru_bias,
    bn_gain,
    bn_shift,
    w_score,
):
    me = lax.axis_index("dom")
    group = lax.axis_index("epoch")
    after = lax.rem(group + 1, groups)
    ahead = lax.rem(group + groups - 1, groups)
    nodes, width = table.shape
    events = feat.shape[0]
    slots = parts * CAP
    hsize = width // HEADS
    rings = parts // PLANE
    layer = rings * CORES
    y, inner = lax.div(me, layer), lax.rem(me, layer)
    z, core = lax.div(inner, CORES), lax.rem(inner, CORES)
    spot = y * CORES + core
    offsets = []
    for by in range(PLANE):
        there = lax.rem(spot + by, PLANE)
        offsets.append(lax.div(there, CORES) * layer + lax.rem(there, CORES))

    held = (
        table,
        nbr,
        own,
        row,
        feat,
        lab,
        w_query,
        w_keyval,
        w_out,
        w_msg_mem,
        w_msg_edge,
        w_pair_edge,
        gru_input,
        gru_hidden,
        gru_bias,
        bn_gain,
        bn_shift,
        w_score,
    )
    given = (
        table_h,
        nbr_h,
        own_h,
        row_h,
        feat_h,
        lab_h,
        w_query_h,
        w_keyval_h,
        w_out_h,
        w_msg_mem_h,
        w_msg_edge_h,
        w_pair_edge_h,
        gru_input_h,
        gru_hidden_h,
        gru_bias_h,
        bn_gain_h,
        bn_shift_h,
        w_score_h,
    )
    loads = [
        pltpu.make_async_copy(src, dst, load_sem.at[k])
        for k, (src, dst) in enumerate(zip(given, held))
    ]
    for k in LOAD_ORDER:
        loads[k].start()

    barrier = pltpu.get_barrier_semaphore()

    def each_turn(visit, first, last):
        if first == 0:
            visit(0)
        top = min(last, rings - 1)

        def one(turn, carry):
            visit(turn)
            return carry

        lax.fori_loop(max(first, 1), top, one, 0)
        if last == rings:
            visit(rings - 1)

    def each_peer(turn):
        base = lax.rem(z + along(turn, rings), rings) * CORES
        own_turn = isinstance(turn, int) and turn == rings - 1
        return [(by, base + offsets[by]) for by in range(1 if own_turn else 0, PLANE)]

    def greet(turn):
        for _, peer in each_peer(turn):
            pl.semaphore_signal(barrier, inc=1, device_id={"dom": peer}, device_id_type=MESH)

    each_turn(greet, 0, rings)
    pl.semaphore_signal(barrier, inc=1, device_id={"epoch": ahead}, device_id_type=MESH)

    def remote(src, dst, sent, received, peer):
        return pltpu.make_async_remote_copy(
            src_ref=src,
            dst_ref=dst,
            send_sem=sent,
            recv_sem=received,
            device_id={"dom": peer},
            device_id_type=MESH,
        )

    def send_turns(src, dst, which, first, last):
        def visit(turn):
            back = facing(turn, rings)
            for by, peer in each_peer(turn):
                remote(
                    src.at[turn * PLANE + by],
                    dst.at[back * PLANE + (PLANE - by) % PLANE],
                    send_sem.at[which],
                    recv_sem.at[which, lax.div(back, TURNS)],
                    peer,
                ).start()

        each_turn(visit, first, last)
        if last == rings:
            here = (rings - 1) * PLANE
            pltpu.make_async_copy(
                src.at[here], dst.at[here], recv_sem.at[which, GROUPS - 1]
            ).start()

    def send_groups(src, dst, which, first, last):
        send_turns(src, dst, which, first * TURNS, last * TURNS)

    def wait_group(dst, which, g):
        block = dst.at[pl.ds(g * TURNS * PLANE, TURNS * PLANE)]
        pltpu.make_async_copy(block, block, recv_sem.at[which, g]).wait()

    def wait_sent(dst, which):
        sent = dst.at[pl.ds(0, parts - 1)]
        pltpu.make_async_copy(sent, sent, send_sem.at[which]).wait()

    loads[2].wait()
    loads[3].wait()
    ends = 2 * events
    o = jnp.concatenate([own[0:1, :], own[1:2, :]], axis=1)
    r = jnp.concatenate([row[0:1, :], row[1:2, :]], axis=1) + 1
    away = (o // CORES - z + parts) % rings
    away = jnp.where(away == 0, rings // 2, away - rings // 2)
    turn_of = jnp.where(away > 0, 2 * away - 1, -2 * away)
    o = turn_of * PLANE + (o // layer * CORES + o % CORES - spot + PLANE) % PLANE
    owned = iota((parts, ends), 0) == o
    owned_b = onehot(owned)
    earlier = onehot(iota((ends, ends), 0) < iota((ends, ends), 1))
    before = dot(owned_b, earlier)
    rank = jnp.sum(jnp.where(owned, before, 0.0), axis=0, keepdims=True)
    rank_i = rank.astype(jnp.int32)
    ranked = iota((LANES, ends), 0) == rank_i
    high = jnp.where(ranked, (r // 32).astype(F32), 0.0).astype(BF16)
    low = jnp.where(ranked, (r % 32).astype(F32), 0.0).astype(BF16)
    asked = dot_nt(owned_b, high) * 32.0 + dot_nt(owned_b, low)
    req_s[...] = asked.reshape(parts, 1, LANES)

    pl.semaphore_wait(barrier, parts)
    send_groups(req_s, req_r, 0, 0, GROUPS)

    place = o * CAP + rank_i
    place_s[...] = onehot(iota((slots, ends), 0) == place)
    diagonal = iota((ends, ends), 0) == iota((ends, ends), 1)
    place_col = jnp.sum(jnp.where(diagonal, place.astype(F32), 0.0), axis=1, keepdims=True)
    place_t[...] = onehot(iota((ends, slots), 1) == place_col.astype(jnp.int32))

    for k in (0, 1, 6, 7, 8):
        loads[k].wait()
    keyval[...] = dot(table[...], w_keyval[...]).astype(BF16)
    query[...] = dot(table[...], w_query[...]).astype(BF16)
    block = LANES
    scale = 1.0 / jnp.sqrt(jnp.float32(hsize))
    for b in range(nodes // block):
        here = pl.ds(b * block, block)
        times = jnp.zeros((nodes, block), F32)
        for j in range(nbr.shape[0]):
            times = times + jnp.where(iota((nodes, block), 0) == nbr[j : j + 1, here], 1.0, 0.0)
        for h in range(HEADS):
            cols = pl.ds(h * hsize, hsize)
            score = dot_nt(keyval[:, cols], query[here, cols]) * scale
            score = jnp.where(times > 0, score, -1e30)
            top = jnp.max(score, axis=0, keepdims=True)
            grown = jnp.exp(score - top)
            total = jnp.sum(grown * times, axis=0, keepdims=True)
            weight = (grown / total).astype(BF16).astype(F32) * times
            main = weight.astype(BF16)
            rest = (weight - main.astype(F32)).astype(BF16)
            value = keyval[:, pl.ds(width + h * hsize, hsize)]
            attended[here, cols] = (dot_tn(main, value) + dot_tn(rest, value)).astype(BF16)
    embed[...] = (table[...].astype(F32) + dot(attended[...], w_out[...])).astype(BF16)

    gslots = slots // GROUPS
    gblocks = parts // GROUPS
    mine = iota((gblocks, CAP, LANES), 1) == iota((gblocks, CAP, LANES), 2)
    asked_for = {}
    for g in ORDER_M:
        here, blocks = pl.ds(g * gslots, gslots), pl.ds(g * gblocks, gblocks)
        wait_group(req_r, 0, g)
        got = jnp.broadcast_to(req_r[blocks], (gblocks, CAP, LANES))
        wanted = jnp.sum(jnp.where(mine, got, 0.0), axis=2, keepdims=True).reshape(gslots, 1)
        asked_for[g] = wanted
        pick[here, :] = onehot(iota((gslots, nodes), 1) + 1 == wanted.astype(jnp.int32))
        mem_s[blocks] = pack(dot(pick[here, :], table[...]))
        send_groups(mem_s, mem_r, 1, g, g + 1)
    for g in ORDER_E:
        here, blocks = pl.ds(g * gslots, gslots), pl.ds(g * gblocks, gblocks)
        emb_s[blocks] = pack(dot(pick[here, :], embed[...]))
        send_groups(emb_s, emb_r, 2, g, g + 1)

    for k in (4, 5, 9, 10, 11, 12, 13, 14, 15, 16, 17):
        loads[k].wait()
    wanted = jnp.concatenate([asked_for[g] for g in range(GROUPS)], axis=0)
    square = iota((slots, slots), 0) == iota((slots, slots), 1)
    wanted_row = jnp.sum(jnp.where(square, wanted, 0.0), axis=0, keepdims=True)
    pick_t[...] = onehot(iota((nodes, slots), 0) + 1 == wanted_row.astype(jnp.int32))
    times_named[...] = dot(pick_t[...], jnp.ones((slots, LANES), BF16))
    hidden[...] = dot(table[...], gru_hidden[...])
    msg_edge = dot(feat[...], w_msg_edge[...])
    pair_edge = dot(feat[...], w_pair_edge[...])

    rows_back = jnp.zeros((ends, width), F32)
    for g in range(GROUPS):
        wait_group(mem_r, 1, g)
        blocks = pl.ds(g * gblocks, gblocks)
        rows_back = rows_back + dot(
            place_t[:, pl.ds(g * gslots, gslots)], unpack(mem_r[blocks])
        )
    rows_back = rows_back.astype(BF16)
    to_src = dot(rows_back[events:], w_msg_mem[...]) + msg_edge
    to_dst = dot(rows_back[:events], w_msg_mem[...]) + msg_edge
    message = jnp.concatenate([to_src, to_dst], axis=0).astype(BF16)
    for g in range(GROUPS):
        blocks = pl.ds(g * gblocks, gblocks)
        msg_s[blocks] = pack(dot(place_s[pl.ds(g * gslots, gslots), :], message))
        if g < EARLY:
            send_groups(msg_s, msg_r, 3, g, g + 1)

    ends_back = jnp.zeros((ends, width), F32)
    for g in range(GROUPS):
        wait_group(emb_r, 2, g)
        blocks = pl.ds(g * gblocks, gblocks)
        ends_back = ends_back + dot(
            place_t[:, pl.ds(g * gslots, gslots)], unpack(emb_r[blocks])
        )
    pair = ends_back[:events] * ends_back[events:] + pair_edge
    sum_one = jnp.sum(pair, axis=0, keepdims=True)
    sum_two = jnp.sum(pair * pair, axis=0, keepdims=True)
    st_r[pl.ds(spot, 1)] = jnp.concatenate([sum_one, sum_two], axis=1).reshape(1, 1, 2 * width)
    copies = []
    for by in range(1, PLANE):
        copies.append(
            remote(
                st_r.at[spot],
                st_r.at[spot],
                st_send.at[by - 1],
                st_recv.at[PLANE - 1 - by],
                z * CORES + offsets[by],
            )
        )
    for copy in copies:
        copy.start()
    for by in range(1, PLANE):
        other = lax.rem(spot + by, PLANE)
        remote(
            st_r.at[other], st_r.at[other], st_send.at[by - 1], st_recv.at[by - 1], me
        ).wait_recv()
    plane_sum = st_r[0:1] + st_r[1:2] + st_r[2:3] + st_r[3:4]
    tot_r[pl.ds(z, 1)] = plane_sum

    def spread_sums(step, carry):
        peer = lax.rem(z + step, rings) * CORES + offsets[0]
        remote(tot_r.at[z], tot_r.at[z], send_sem.at[4], tot_sem, peer).start()
        return carry

    lax.fori_loop(1, rings, spread_sums, 0)
    if EARLY < GROUPS:
        send_groups(msg_s, msg_r, 3, EARLY, GROUPS)

    others = tot_r.at[pl.ds(0, rings - 1)]
    pltpu.make_async_copy(others, others, tot_sem).wait()
    sums = tot_r[0]
    for k in range(1, rings):
        sums = sums + tot_r[k]
    count_all = jnp.float32(events * parts)
    mean = sums[:, :width] / count_all
    var = sums[:, width:] / count_all - mean * mean
    normed = (pair - mean) * lax.rsqrt(var + 1e-05) * bn_gain[...] + bn_shift[...]
    weighed = jnp.maximum(normed, 0.0) * w_score[...].astype(F32).reshape(1, width)
    logit_col = jnp.sum(weighed, axis=1, keepdims=True)
    corner = iota((events, events), 0) == iota((events, events), 1)
    logit = jnp.sum(jnp.where(corner, logit_col, 0.0), axis=0, keepdims=True)
    soft = jnp.maximum(logit, 0.0) + jnp.log1p(jnp.exp(-jnp.abs(logit)))
    terms = soft - lab[...].astype(F32) * logit
    part = jnp.sum(terms, axis=1, keepdims=True)
    ls_r[pl.ds(me, 1)] = jnp.broadcast_to(part, (1, LANES)).reshape(1, 1, LANES)

    def spread_loss(turn):
        for _, peer in each_peer(turn):
            remote(ls_r.at[me], ls_r.at[me], send_sem.at[5], ls_sem, peer).start()

    each_turn(spread_loss, 0, rings)

    chunk = nodes // NODE_CHUNKS
    for g in range(GROUPS - 1):
        wait_group(msg_r, 3, g)
        blocks = pl.ds(g * gblocks, gblocks)
        part = dot(pick_t[:, pl.ds(g * gslots, gslots)], unpack(msg_r[blocks]))
        agg[...] = part if g == 0 else agg[...] + part
    wait_group(msg_r, 3, GROUPS - 1)
    inbox = unpack(msg_r[pl.ds(parts - gblocks, gblocks)])
    hands = []
    for c in range(NODE_CHUNKS):
        here = pl.ds(c * chunk, chunk)
        count = jnp.concatenate([times_named[here, :], times_named[here, :]], axis=1)
        total = agg[here, :] + dot(pick_t[here, pl.ds(slots - gslots, gslots)], inbox)
        avg = (total / jnp.maximum(count, 1.0)).astype(BF16)
        inp = dot(avg, gru_input[...]) + gru_bias[...].reshape(1, 3 * width)
        hid = hidden[here, :]
        reset = jax.nn.sigmoid(inp[:, :width] + hid[:, :width])
        update = jax.nn.sigmoid(inp[:, width : 2 * width] + hid[:, width : 2 * width])
        cand = jnp.tanh(inp[:, 2 * width :] + reset * hid[:, 2 * width :])
        fresh = (1.0 - update) * cand + update * table[here, :].astype(F32)
        hand_s[here, :] = jnp.where(count > 0, fresh, UNTOUCHED).astype(BF16)
        hand = pltpu.make_async_remote_copy(
            src_ref=hand_s.at[here],
            dst_ref=hand_r.at[here],
            send_sem=hand_send.at[c],
            recv_sem=hand_recv.at[c],
            device_id={"epoch": after},
            device_id_type=MESH,
        )
        hand.start()
        hands.append(hand)

    for c in range(NODE_CHUNKS):
        here = pl.ds(c * chunk, chunk)
        hands[c].wait()
        handed = hand_r[here, :].astype(F32)
        fresh = hand_s[here, :].astype(F32)
        old = table[here, :].astype(F32)
        prior = jnp.where(jnp.logical_and(handed < UNTOUCHED / 2, group > 0), handed, old)
        out[here, :] = jnp.where(fresh < UNTOUCHED / 2, fresh, prior).astype(BF16)

    others = ls_r.at[pl.ds(0, parts - 1)]
    pltpu.make_async_copy(others, others, ls_sem).wait()
    loss[...] = jnp.sum(ls_r[...], axis=0) / count_all

    wait_sent(req_s, 0)
    wait_sent(mem_s, 1)
    wait_sent(emb_s, 2)
    wait_sent(msg_s, 3)
    for copy in copies:
        copy.wait_send()
    others = tot_r.at[pl.ds(0, rings - 1)]
    pltpu.make_async_copy(others, others, send_sem.at[4]).wait()
    wait_sent(ls_r, 5)


def shards(
    parts,
    groups,
    memory,
    neighbours,
    owners,
    rows,
    edge_feat,
    labels,
    w_query,
    w_keyval,
    w_out,
    w_msg_mem,
    w_msg_edge,
    w_pair_edge,
    gru_input,
    gru_hidden,
    gru_bias,
    bn_gain,
    bn_shift,
    w_score,
):
    nodes, width = memory.shape[1:]
    events = owners.shape[1]
    slots = parts * CAP
    ends = 2 * events
    block = (parts, 2 * CAP, LANES)
    line = (parts, 1, LANES)
    operands = (
        memory[0],
        neighbours.T,
        owners[0].T,
        rows[0].T,
        edge_feat[0],
        labels,
        w_query,
        w_keyval,
        w_out,
        w_msg_mem,
        w_msg_edge,
        w_pair_edge,
        gru_input,
        gru_hidden,
        gru_bias,
        bn_gain[None],
        bn_shift[None],
        w_score,
    )
    result, loss = pl.pallas_call(
        functools.partial(kernel, parts, groups),
        out_shape=(
            pltpu.VMEM((nodes, width), BF16),
            pltpu.VMEM((1, LANES), F32),
        ),
        in_specs=[pl.BlockSpec(memory_space=pl.ANY)] * 18,
        out_specs=(pl.BlockSpec(memory_space=pltpu.VMEM),) * 2,
        scratch_shapes=[
            pltpu.VMEM(line, F32),
            pltpu.VMEM(line, F32),
            pltpu.VMEM(block, BF16),
            pltpu.VMEM(block, BF16),
            pltpu.VMEM(block, BF16),
            pltpu.VMEM(block, BF16),
            pltpu.VMEM(block, BF16),
            pltpu.VMEM(block, BF16),
            pltpu.VMEM((PLANE, 1, 2 * width), F32),
            pltpu.VMEM((parts // PLANE, 1, 2 * width), F32),
            pltpu.VMEM(line, F32),
            pltpu.VMEM((nodes, width), BF16),
            pltpu.VMEM((nodes, width), BF16),
            pltpu.VMEM((nodes, 2 * width), BF16),
            pltpu.VMEM((nodes, width), BF16),
            pltpu.VMEM((nodes, width), BF16),
            pltpu.VMEM((nodes, width), BF16),
            pltpu.VMEM((nodes, 3 * width), F32),
            pltpu.VMEM((slots, nodes), BF16),
            pltpu.VMEM((nodes, slots), BF16),
            pltpu.VMEM((slots, ends), BF16),
            pltpu.VMEM((ends, slots), BF16),
            pltpu.VMEM((nodes, LANES), F32),
            pltpu.VMEM((nodes, width), F32),
            pltpu.SemaphoreType.DMA((6,)),
            pltpu.SemaphoreType.DMA((4, GROUPS)),
            pltpu.SemaphoreType.DMA,
            pltpu.SemaphoreType.DMA,
            pltpu.SemaphoreType.DMA((PLANE - 1,)),
            pltpu.SemaphoreType.DMA((PLANE - 1,)),
            pltpu.SemaphoreType.DMA((NODE_CHUNKS,)),
            pltpu.SemaphoreType.DMA((NODE_CHUNKS,)),
            pltpu.SemaphoreType.DMA((len(operands),)),
        ]
        + [pltpu.VMEM(x.shape, x.dtype) for x in operands],
        compiler_params=pltpu.CompilerParams(
            collective_id=0, has_side_effects=True, vmem_limit_bytes=VMEM_LIMIT
        ),
        name="window",
    )(*operands)
    return result[None], loss[0, :1]


def solution(mesh):
    parts, groups = mesh.shape["dom"], mesh.shape["epoch"]
    return jax.shard_map(
        functools.partial(shards, parts, groups),
        mesh=mesh,
        in_specs=(
            P("epoch", "dom", None),
            P("dom", None),
            P("epoch", "dom", None),
            P("epoch", "dom", None),
            P("epoch", "dom", None),
            P("epoch", "dom"),
            P(),
            P(),
            P(),
            P(),
            P(),
            P(),
            P(),
            P(),
            P(),
            P(),
            P(),
            P(),
        ),
        out_specs=(P("epoch", "dom", None), P("epoch")),
        check_vma=False,
    )
```

```python
import functools

import jax
import jax.numpy as jnp
from jax import lax
from jax.experimental import pallas as pl
from jax.experimental.pallas import tpu as pltpu
from jax.sharding import PartitionSpec as P

MESH = pl.DeviceIdType.MESH
F32 = jnp.float32
BF16 = jnp.bfloat16
VMEM_LIMIT = 62 * 1024 * 1024
CAP = 8
HEADS = 2
LANES = 128
CORES = 2
HALVES = 2
PLANE = CORES * HALVES
UNTOUCHED = 1e30
NODE_CHUNKS = 4
ORDER_M = (3, 2, 0, 1)
ORDER_E = (0, 1, 2, 3)
NEAR = 7
GROUPS = 4
TURNS = 4
EARLY = 3
LOAD_ORDER = (2, 3, 0, 7, 1, 6, 8, 4, 10, 9, 11, 13, 12, 14, 15, 16, 17, 5)


def iota(shape, dim):
    return lax.broadcasted_iota(jnp.int32, shape, dim)


def dot(a, b):
    return jnp.dot(a, b, preferred_element_type=F32)


def dot_nt(a, b):
    return lax.dot_general(a, b, (((1,), (1,)), ((), ())), preferred_element_type=F32)


def dot_tn(a, b):
    return lax.dot_general(a, b, (((0,), (0,)), ((), ())), preferred_element_type=F32)


def onehot(mask):
    return jnp.where(mask, 1.0, 0.0).astype(BF16)


def pack(x):
    rows = x.shape[0] // CAP
    left = x[:, :LANES].reshape(rows, CAP, LANES)
    right = x[:, LANES:].reshape(rows, CAP, LANES)
    return jnp.concatenate([left, right], axis=1).astype(BF16)


def unpack(x):
    rows = x.shape[0]
    x = x.astype(F32)
    left = x[:, :CAP].reshape(rows * CAP, LANES)
    right = x[:, CAP:].reshape(rows * CAP, LANES)
    return jnp.concatenate([left, right], axis=1).astype(BF16)


def along(turn, rings):
    half = (turn + 1) // 2
    if isinstance(turn, int):
        return rings // 2 + (half if turn % 2 else rings - half)
    return rings // 2 + jnp.where(lax.rem(turn, 2) == 1, half, rings - half)


def facing(turn, rings):
    if isinstance(turn, int):
        if turn in (0, rings - 1):
            return turn
        return turn + 1 if turn % 2 else turn - 1
    return turn + jnp.where(lax.rem(turn, 2) == 1, 1, -1)


def halfway(turn, rings):
    return rings // 4 if turn % 2 == 0 else rings - rings // 4


def kernel(
    parts,
    groups,
    table_h,
    nbr_h,
    own_h,
    row_h,
    feat_h,
    lab_h,
    w_query_h,
    w_keyval_h,
    w_out_h,
    w_msg_mem_h,
    w_msg_edge_h,
    w_pair_edge_h,
    gru_input_h,
    gru_hidden_h,
    gru_bias_h,
    bn_gain_h,
    bn_shift_h,
    w_score_h,
    out,
    loss,
    req_s,
    req_r,
    mem_s,
    mem_r,
    emb_s,
    emb_r,
    msg_s,
    msg_r,
    st_r,
    tot_r,
    ls_r,
    hand_s,
    hand_r,
    keyval,
    query,
    attended,
    embed,
    hidden,
    pick,
    pick_t,
    place_s,
    place_t,
    times_named,
    agg,
    send_sem,
    recv_sem,
    relay,
    relay_send,
    relay_recv,
    tot_sem,
    ls_sem,
    st_send,
    st_recv,
    hand_send,
    hand_recv,
    load_sem,
    table,
    nbr,
    own,
    row,
    feat,
    lab,
    w_query,
    w_keyval,
    w_out,
    w_msg_mem,
    w_msg_edge,
    w_pair_edge,
    gru_input,
    gru_hidden,
    gru_bias,
    bn_gain,
    bn_shift,
    w_score,
):
    me = lax.axis_index("dom")
    group = lax.axis_index("epoch")
    after = lax.rem(group + 1, groups)
    ahead = lax.rem(group + groups - 1, groups)
    nodes, width = table.shape
    events = feat.shape[0]
    slots = parts * CAP
    hsize = width // HEADS
    rings = parts // PLANE
    layer = rings * CORES
    y, inner = lax.div(me, layer), lax.rem(me, layer)
    z, core = lax.div(inner, CORES), lax.rem(inner, CORES)
    spot = y * CORES + core
    offsets = []
    for by in range(PLANE):
        there = lax.rem(spot + by, PLANE)
        offsets.append(lax.div(there, CORES) * layer + lax.rem(there, CORES))

    held = (
        table,
        nbr,
        own,
        row,
        feat,
        lab,
        w_query,
        w_keyval,
        w_out,
        w_msg_mem,
        w_msg_edge,
        w_pair_edge,
        gru_input,
        gru_hidden,
        gru_bias,
        bn_gain,
        bn_shift,
        w_score,
    )
    given = (
        table_h,
        nbr_h,
        own_h,
        row_h,
        feat_h,
        lab_h,
        w_query_h,
        w_keyval_h,
        w_out_h,
        w_msg_mem_h,
        w_msg_edge_h,
        w_pair_edge_h,
        gru_input_h,
        gru_hidden_h,
        gru_bias_h,
        bn_gain_h,
        bn_shift_h,
        w_score_h,
    )
    loads = [
        pltpu.make_async_copy(src, dst, load_sem.at[k])
        for k, (src, dst) in enumerate(zip(given, held))
    ]
    for k in LOAD_ORDER[:2]:
        loads[k].start()

    barrier = pltpu.get_barrier_semaphore()

    def each_turn(visit, first, last):
        if first == 0:
            visit(0)
        top = min(last, rings - 1)

        def one(turn, carry):
            visit(turn)
            return carry

        lax.fori_loop(max(first, 1), top, one, 0)
        if last == rings:
            visit(rings - 1)

    def each_peer(turn):
        base = lax.rem(z + along(turn, rings), rings) * CORES
        own_turn = isinstance(turn, int) and turn == rings - 1
        return [(by, base + offsets[by]) for by in range(1 if own_turn else 0, PLANE)]

    def greet(turn):
        for _, peer in each_peer(turn):
            pl.semaphore_signal(barrier, inc=1, device_id={"dom": peer}, device_id_type=MESH)

    each_turn(greet, NEAR, rings)
    pl.semaphore_signal(barrier, inc=1, device_id={"epoch": ahead}, device_id_type=MESH)
    for k in LOAD_ORDER[2:]:
        loads[k].start()

    def remote(src, dst, sent, received, peer):
        return pltpu.make_async_remote_copy(
            src_ref=src,
            dst_ref=dst,
            send_sem=sent,
            recv_sem=received,
            device_id={"dom": peer},
            device_id_type=MESH,
        )

    def send_turns(src, dst, which, first, last):
        def visit(turn):
            back = facing(turn, rings)
            for by, peer in each_peer(turn):
                remote(
                    src.at[turn * PLANE + by],
                    dst.at[back * PLANE + (PLANE - by) % PLANE],
                    send_sem.at[which],
                    recv_sem.at[which, lax.div(back, TURNS)],
                    peer,
                ).start()

        each_turn(visit, first, last)
        if last == rings:
            here = (rings - 1) * PLANE
            pltpu.make_async_copy(
                src.at[here], dst.at[here], recv_sem.at[which, GROUPS - 1]
            ).start()

    def send_groups(src, dst, which, first, last):
        send_turns(src, dst, which, first * TURNS, last * TURNS)

    def wait_group(dst, which, g):
        block = dst.at[pl.ds(g * TURNS * PLANE, TURNS * PLANE)]
        pltpu.make_async_copy(block, block, recv_sem.at[which, g]).wait()

    def wait_sent(dst, which):
        sent = dst.at[pl.ds(0, parts - 1)]
        pltpu.make_async_copy(sent, sent, send_sem.at[which]).wait()

    loads[2].wait()
    loads[3].wait()
    ends = 2 * events
    o = jnp.concatenate([own[0:1, :], own[1:2, :]], axis=1)
    r = jnp.concatenate([row[0:1, :], row[1:2, :]], axis=1) + 1
    away = (o // CORES - z + parts) % rings
    away = jnp.where(away == 0, rings // 2, away - rings // 2)
    turn_of = jnp.where(away > 0, 2 * away - 1, -2 * away)
    o = turn_of * PLANE + (o // layer * CORES + o % CORES - spot + PLANE) % PLANE
    owned = iota((parts, ends), 0) == o
    owned_b = onehot(owned)
    earlier = onehot(iota((ends, ends), 0) < iota((ends, ends), 1))
    before = dot(owned_b, earlier)
    rank = jnp.sum(jnp.where(owned, before, 0.0), axis=0, keepdims=True)
    rank_i = rank.astype(jnp.int32)
    ranked = iota((LANES, ends), 0) == rank_i
    high = jnp.where(ranked, (r // 32).astype(F32), 0.0).astype(BF16)
    low = jnp.where(ranked, (r % 32).astype(F32), 0.0).astype(BF16)
    asked = dot_nt(owned_b, high) * 32.0 + dot_nt(owned_b, low)
    req_s[...] = asked.reshape(parts, 1, LANES)

    pl.semaphore_wait(barrier, (rings - NEAR) * PLANE)
    for turn in range(NEAR):
        blocks = pl.ds(turn * PLANE, PLANE)
        peer = lax.rem(z + halfway(turn, rings), rings) * CORES + offsets[0]
        remote(req_s.at[blocks], relay.at[blocks], relay_send, relay_recv, peer).start()
    send_turns(req_s, req_r, 0, NEAR, rings)

    place = o * CAP + rank_i
    place_s[...] = onehot(iota((slots, ends), 0) == place)
    diagonal = iota((ends, ends), 0) == iota((ends, ends), 1)
    place_col = jnp.sum(jnp.where(diagonal, place.astype(F32), 0.0), axis=1, keepdims=True)
    place_t[...] = onehot(iota((ends, slots), 1) == place_col.astype(jnp.int32))

    for k in (0, 1, 6, 7, 8):
        loads[k].wait()
    keyval[...] = dot(table[...], w_keyval[...]).astype(BF16)
    query[...] = dot(table[...], w_query[...]).astype(BF16)

    pltpu.make_async_copy(relay, relay, relay_recv).wait()
    for turn in range(NEAR):
        onward = along(turn, rings) - halfway(turn, rings) + rings
        base = lax.rem(z + onward, rings) * CORES
        back = facing(turn, rings)
        for by in range(PLANE):
            remote(
                relay.at[turn * PLANE + by],
                req_r.at[back * PLANE + (PLANE - by) % PLANE],
                send_sem.at[0],
                recv_sem.at[0, back // TURNS],
                base + offsets[by],
            ).start()

    gslots = slots // GROUPS
    gblocks = parts // GROUPS
    mine = iota((gblocks, CAP, LANES), 1) == iota((gblocks, CAP, LANES), 2)
    asked_for = {}
    for g in ORDER_M:
        here, blocks = pl.ds(g * gslots, gslots), pl.ds(g * gblocks, gblocks)
        wait_group(req_r, 0, g)
        got = jnp.broadcast_to(req_r[blocks], (gblocks, CAP, LANES))
        wanted = jnp.sum(jnp.where(mine, got, 0.0), axis=2, keepdims=True).reshape(gslots, 1)
        asked_for[g] = wanted
        pick[here, :] = onehot(iota((gslots, nodes), 1) + 1 == wanted.astype(jnp.int32))
        mem_s[blocks] = pack(dot(pick[here, :], table[...]))
        send_groups(mem_s, mem_r, 1, g, g + 1)
    block = LANES
    scale = 1.0 / jnp.sqrt(jnp.float32(hsize))
    for b in range(nodes // block):
        here = pl.ds(b * block, block)
        times = jnp.zeros((nodes, block), F32)
        for j in range(nbr.shape[0]):
            times = times + jnp.where(iota((nodes, block), 0) == nbr[j : j + 1, here], 1.0, 0.0)
        for h in range(HEADS):
            cols = pl.ds(h * hsize, hsize)
            score = dot_nt(keyval[:, cols], query[here, cols]) * scale
            score = jnp.where(times > 0, score, -1e30)
            top = jnp.max(score, axis=0, keepdims=True)
            grown = jnp.exp(score - top)
            total = jnp.sum(grown * times, axis=0, keepdims=True)
            weight = (grown / total).astype(BF16).astype(F32) * times
            main = weight.astype(BF16)
            rest = (weight - main.astype(F32)).astype(BF16)
            value = keyval[:, pl.ds(width + h * hsize, hsize)]
            attended[here, cols] = (dot_tn(main, value) + dot_tn(rest, value)).astype(BF16)
    embed[...] = (table[...].astype(F32) + dot(attended[...], w_out[...])).astype(BF16)

    for g in ORDER_E:
        here, blocks = pl.ds(g * gslots, gslots), pl.ds(g * gblocks, gblocks)
        emb_s[blocks] = pack(dot(pick[here, :], embed[...]))
        send_groups(emb_s, emb_r, 2, g, g + 1)

    for k in (4, 5, 9, 10, 11, 12, 13, 14, 15, 16, 17):
        loads[k].wait()
    wanted = jnp.concatenate([asked_for[g] for g in range(GROUPS)], axis=0)
    square = iota((slots, slots), 0) == iota((slots, slots), 1)
    wanted_row = jnp.sum(jnp.where(square, wanted, 0.0), axis=0, keepdims=True)
    pick_t[...] = onehot(iota((nodes, slots), 0) + 1 == wanted_row.astype(jnp.int32))
    times_named[...] = dot(pick_t[...], jnp.ones((slots, LANES), BF16))
    hidden[...] = dot(table[...], gru_hidden[...])
    msg_edge = dot(feat[...], w_msg_edge[...])
    pair_edge = dot(feat[...], w_pair_edge[...])

    rows_back = jnp.zeros((ends, width), F32)
    for g in range(GROUPS):
        wait_group(mem_r, 1, g)
        blocks = pl.ds(g * gblocks, gblocks)
        rows_back = rows_back + dot(
            place_t[:, pl.ds(g * gslots, gslots)], unpack(mem_r[blocks])
        )
    rows_back = rows_back.astype(BF16)
    to_src = dot(rows_back[events:], w_msg_mem[...]) + msg_edge
    to_dst = dot(rows_back[:events], w_msg_mem[...]) + msg_edge
    message = jnp.concatenate([to_src, to_dst], axis=0).astype(BF16)
    for g in range(GROUPS):
        blocks = pl.ds(g * gblocks, gblocks)
        msg_s[blocks] = pack(dot(place_s[pl.ds(g * gslots, gslots), :], message))
        if g < EARLY:
            send_groups(msg_s, msg_r, 3, g, g + 1)

    ends_back = jnp.zeros((ends, width), F32)
    for g in range(GROUPS):
        wait_group(emb_r, 2, g)
        blocks = pl.ds(g * gblocks, gblocks)
        ends_back = ends_back + dot(
            place_t[:, pl.ds(g * gslots, gslots)], unpack(emb_r[blocks])
        )
    pair = ends_back[:events] * ends_back[events:] + pair_edge
    sum_one = jnp.sum(pair, axis=0, keepdims=True)
    sum_two = jnp.sum(pair * pair, axis=0, keepdims=True)
    st_r[pl.ds(spot, 1)] = jnp.concatenate([sum_one, sum_two], axis=1).reshape(1, 1, 2 * width)
    copies = []
    for by in range(1, PLANE):
        copies.append(
            remote(
                st_r.at[spot],
                st_r.at[spot],
                st_send.at[by - 1],
                st_recv.at[PLANE - 1 - by],
                z * CORES + offsets[by],
            )
        )
    for copy in copies:
        copy.start()
    for by in range(1, PLANE):
        other = lax.rem(spot + by, PLANE)
        remote(
            st_r.at[other], st_r.at[other], st_send.at[by - 1], st_recv.at[by - 1], me
        ).wait_recv()
    plane_sum = st_r[0:1] + st_r[1:2] + st_r[2:3] + st_r[3:4]
    tot_r[pl.ds(z, 1)] = plane_sum

    def spread_sums(step, carry):
        peer = lax.rem(z + step, rings) * CORES + offsets[0]
        remote(tot_r.at[z], tot_r.at[z], send_sem.at[4], tot_sem, peer).start()
        return carry

    lax.fori_loop(1, rings, spread_sums, 0)
    if EARLY < GROUPS:
        send_groups(msg_s, msg_r, 3, EARLY, GROUPS)

    chunk = nodes // NODE_CHUNKS
    for g in range(GROUPS - 1):
        wait_group(msg_r, 3, g)
        blocks = pl.ds(g * gblocks, gblocks)
        part = dot(pick_t[:, pl.ds(g * gslots, gslots)], unpack(msg_r[blocks]))
        agg[...] = part if g == 0 else agg[...] + part
    wait_group(msg_r, 3, GROUPS - 1)
    inbox = unpack(msg_r[pl.ds(parts - gblocks, gblocks)])
    hands = []
    for c in range(NODE_CHUNKS):
        here = pl.ds(c * chunk, chunk)
        count = jnp.concatenate([times_named[here, :], times_named[here, :]], axis=1)
        total = agg[here, :] + dot(pick_t[here, pl.ds(slots - gslots, gslots)], inbox)
        avg = (total / jnp.maximum(count, 1.0)).astype(BF16)
        inp = dot(avg, gru_input[...]) + gru_bias[...].reshape(1, 3 * width)
        hid = hidden[here, :]
        reset = jax.nn.sigmoid(inp[:, :width] + hid[:, :width])
        update = jax.nn.sigmoid(inp[:, width : 2 * width] + hid[:, width : 2 * width])
        cand = jnp.tanh(inp[:, 2 * width :] + reset * hid[:, 2 * width :])
        fresh = (1.0 - update) * cand + update * table[here, :].astype(F32)
        hand_s[here, :] = jnp.where(count > 0, fresh, UNTOUCHED).astype(BF16)
        hand = pltpu.make_async_remote_copy(
            src_ref=hand_s.at[here],
            dst_ref=hand_r.at[here],
            send_sem=hand_send.at[c],
            recv_sem=hand_recv.at[c],
            device_id={"epoch": after},
            device_id_type=MESH,
        )
        hand.start()
        hands.append(hand)

    others = tot_r.at[pl.ds(0, rings - 1)]
    pltpu.make_async_copy(others, others, tot_sem).wait()
    sums = tot_r[0]
    for k in range(1, rings):
        sums = sums + tot_r[k]
    count_all = jnp.float32(events * parts)
    mean = sums[:, :width] / count_all
    var = sums[:, width:] / count_all - mean * mean
    normed = (pair - mean) * lax.rsqrt(var + 1e-05) * bn_gain[...] + bn_shift[...]
    weighed = jnp.maximum(normed, 0.0) * w_score[...].astype(F32).reshape(1, width)
    logit_col = jnp.sum(weighed, axis=1, keepdims=True)
    corner = iota((events, events), 0) == iota((events, events), 1)
    logit = jnp.sum(jnp.where(corner, logit_col, 0.0), axis=0, keepdims=True)
    soft = jnp.maximum(logit, 0.0) + jnp.log1p(jnp.exp(-jnp.abs(logit)))
    terms = soft - lab[...].astype(F32) * logit
    part = jnp.sum(terms, axis=1, keepdims=True)
    ls_r[pl.ds(me, 1)] = jnp.broadcast_to(part, (1, LANES)).reshape(1, 1, LANES)

    def spread_loss(turn):
        for _, peer in each_peer(turn):
            remote(ls_r.at[me], ls_r.at[me], send_sem.at[5], ls_sem, peer).start()

    each_turn(spread_loss, 0, rings)

    for c in range(NODE_CHUNKS):
        here = pl.ds(c * chunk, chunk)
        hands[c].wait()
        handed = hand_r[here, :].astype(F32)
        fresh = hand_s[here, :].astype(F32)
        old = table[here, :].astype(F32)
        prior = jnp.where(jnp.logical_and(handed < UNTOUCHED / 2, group > 0), handed, old)
        out[here, :] = jnp.where(fresh < UNTOUCHED / 2, fresh, prior).astype(BF16)

    others = ls_r.at[pl.ds(0, parts - 1)]
    pltpu.make_async_copy(others, others, ls_sem).wait()
    loss[...] = jnp.sum(ls_r[...], axis=0) / count_all

    wait_sent(req_s, 0)
    pltpu.make_async_copy(relay, relay, relay_send).wait()
    wait_sent(mem_s, 1)
    wait_sent(emb_s, 2)
    wait_sent(msg_s, 3)
    for copy in copies:
        copy.wait_send()
    others = tot_r.at[pl.ds(0, rings - 1)]
    pltpu.make_async_copy(others, others, send_sem.at[4]).wait()
    wait_sent(ls_r, 5)


def shards(
    parts,
    groups,
    memory,
    neighbours,
    owners,
    rows,
    edge_feat,
    labels,
    w_query,
    w_keyval,
    w_out,
    w_msg_mem,
    w_msg_edge,
    w_pair_edge,
    gru_input,
    gru_hidden,
    gru_bias,
    bn_gain,
    bn_shift,
    w_score,
):
    nodes, width = memory.shape[1:]
    events = owners.shape[1]
    slots = parts * CAP
    ends = 2 * events
    block = (parts, 2 * CAP, LANES)
    line = (parts, 1, LANES)
    operands = (
        memory[0],
        neighbours.T,
        owners[0].T,
        rows[0].T,
        edge_feat[0],
        labels,
        w_query,
        w_keyval,
        w_out,
        w_msg_mem,
        w_msg_edge,
        w_pair_edge,
        gru_input,
        gru_hidden,
        gru_bias,
        bn_gain[None],
        bn_shift[None],
        w_score,
    )
    result, loss = pl.pallas_call(
        functools.partial(kernel, parts, groups),
        out_shape=(
            pltpu.VMEM((nodes, width), BF16),
            pltpu.VMEM((1, LANES), F32),
        ),
        in_specs=[pl.BlockSpec(memory_space=pl.ANY)] * 18,
        out_specs=(pl.BlockSpec(memory_space=pltpu.VMEM),) * 2,
        scratch_shapes=[
            pltpu.VMEM(line, F32),
            pltpu.VMEM(line, F32),
            pltpu.VMEM(block, BF16),
            pltpu.VMEM(block, BF16),
            pltpu.VMEM(block, BF16),
            pltpu.VMEM(block, BF16),
            pltpu.VMEM(block, BF16),
            pltpu.VMEM(block, BF16),
            pltpu.VMEM((PLANE, 1, 2 * width), F32),
            pltpu.VMEM((parts // PLANE, 1, 2 * width), F32),
            pltpu.VMEM(line, F32),
            pltpu.VMEM((nodes, width), BF16),
            pltpu.VMEM((nodes, width), BF16),
            pltpu.VMEM((nodes, 2 * width), BF16),
            pltpu.VMEM((nodes, width), BF16),
            pltpu.VMEM((nodes, width), BF16),
            pltpu.VMEM((nodes, width), BF16),
            pltpu.VMEM((nodes, 3 * width), F32),
            pltpu.VMEM((slots, nodes), BF16),
            pltpu.VMEM((nodes, slots), BF16),
            pltpu.VMEM((slots, ends), BF16),
            pltpu.VMEM((ends, slots), BF16),
            pltpu.VMEM((nodes, LANES), F32),
            pltpu.VMEM((nodes, width), F32),
            pltpu.SemaphoreType.DMA((6,)),
            pltpu.SemaphoreType.DMA((4, GROUPS)),
            pltpu.VMEM((NEAR * PLANE, 1, LANES), F32),
            pltpu.SemaphoreType.DMA,
            pltpu.SemaphoreType.DMA,
            pltpu.SemaphoreType.DMA,
            pltpu.SemaphoreType.DMA,
            pltpu.SemaphoreType.DMA((PLANE - 1,)),
            pltpu.SemaphoreType.DMA((PLANE - 1,)),
            pltpu.SemaphoreType.DMA((NODE_CHUNKS,)),
            pltpu.SemaphoreType.DMA((NODE_CHUNKS,)),
            pltpu.SemaphoreType.DMA((len(operands),)),
        ]
        + [pltpu.VMEM(x.shape, x.dtype) for x in operands],
        compiler_params=pltpu.CompilerParams(
            collective_id=0, has_side_effects=True, vmem_limit_bytes=VMEM_LIMIT
        ),
        name="window",
    )(*operands)
    return result[None], loss[0, :1]


def solution(mesh):
    parts, groups = mesh.shape["dom"], mesh.shape["epoch"]
    return jax.shard_map(
        functools.partial(shards, parts, groups),
        mesh=mesh,
        in_specs=(
            P("epoch", "dom", None),
            P("dom", None),
            P("epoch", "dom", None),
            P("epoch", "dom", None),
            P("epoch", "dom", None),
            P("epoch", "dom"),
            P(),
            P(),
            P(),
            P(),
            P(),
            P(),
            P(),
            P(),
            P(),
            P(),
            P(),
            P(),
        ),
        out_specs=(P("epoch", "dom", None), P("epoch")),
        check_vma=False,
    )
```

```python
import functools

import jax
import jax.numpy as jnp
from jax import lax
from jax.experimental import pallas as pl
from jax.experimental.pallas import tpu as pltpu
from jax.sharding import PartitionSpec as P

MESH = pl.DeviceIdType.MESH
F32 = jnp.float32
BF16 = jnp.bfloat16
VMEM_LIMIT = 62 * 1024 * 1024
CAP = 8
HEADS = 2
LANES = 128
CORES = 2
HALVES = 2
PLANE = CORES * HALVES
UNTOUCHED = 1e30
NODE_CHUNKS = 4
ORDER_M = (3, 2, 0, 1)
ORDER_E = (0, 1, 2, 3)
NEAR = 7
GROUPS = 4
TURNS = 4
EARLY = 3
LOAD_ORDER = (2, 3, 0, 7, 1, 6, 8, 4, 10, 9, 11, 13, 12, 14, 15, 16, 17, 5)


def iota(shape, dim):
    return lax.broadcasted_iota(jnp.int32, shape, dim)


def dot(a, b):
    return jnp.dot(a, b, preferred_element_type=F32)


def dot_nt(a, b):
    return lax.dot_general(a, b, (((1,), (1,)), ((), ())), preferred_element_type=F32)


def dot_tn(a, b):
    return lax.dot_general(a, b, (((0,), (0,)), ((), ())), preferred_element_type=F32)


def onehot(mask):
    return jnp.where(mask, 1.0, 0.0).astype(BF16)


def pack(x):
    rows = x.shape[0] // CAP
    left = x[:, :LANES].reshape(rows, CAP, LANES)
    right = x[:, LANES:].reshape(rows, CAP, LANES)
    return jnp.concatenate([left, right], axis=1).astype(BF16)


def unpack(x):
    rows = x.shape[0]
    x = x.astype(F32)
    left = x[:, :CAP].reshape(rows * CAP, LANES)
    right = x[:, CAP:].reshape(rows * CAP, LANES)
    return jnp.concatenate([left, right], axis=1).astype(BF16)


def along(turn, rings):
    half = (turn + 1) // 2
    if isinstance(turn, int):
        return rings // 2 + (half if turn % 2 else rings - half)
    return rings // 2 + jnp.where(lax.rem(turn, 2) == 1, half, rings - half)


def facing(turn, rings):
    if isinstance(turn, int):
        if turn in (0, rings - 1):
            return turn
        return turn + 1 if turn % 2 else turn - 1
    return turn + jnp.where(lax.rem(turn, 2) == 1, 1, -1)


def halfway(turn, rings):
    return rings // 4 if turn % 2 == 0 else rings - rings // 4


def kernel(
    parts,
    groups,
    table_h,
    nbr_h,
    own_h,
    row_h,
    feat_h,
    lab_h,
    w_query_h,
    w_keyval_h,
    w_out_h,
    w_msg_mem_h,
    w_msg_edge_h,
    w_pair_edge_h,
    gru_input_h,
    gru_hidden_h,
    gru_bias_h,
    bn_gain_h,
    bn_shift_h,
    w_score_h,
    out,
    loss,
    req_s,
    req_r,
    mem_s,
    mem_r,
    emb_s,
    emb_r,
    msg_s,
    msg_r,
    st_r,
    tot_r,
    ls_r,
    hand_s,
    hand_r,
    keyval,
    query,
    attended,
    embed,
    hidden,
    pick,
    pick_t,
    place_s,
    place_t,
    times_named,
    agg,
    send_sem,
    recv_sem,
    relay,
    relay_send,
    relay_recv,
    tot_sem,
    ls_sem,
    st_send,
    st_recv,
    hand_send,
    hand_recv,
    load_sem,
    table,
    nbr,
    own,
    row,
    feat,
    lab,
    w_query,
    w_keyval,
    w_out,
    w_msg_mem,
    w_msg_edge,
    w_pair_edge,
    gru_input,
    gru_hidden,
    gru_bias,
    bn_gain,
    bn_shift,
    w_score,
):
    me = lax.axis_index("dom")
    group = lax.axis_index("epoch")
    after = lax.rem(group + 1, groups)
    ahead = lax.rem(group + groups - 1, groups)
    nodes, width = table.shape
    events = feat.shape[0]
    slots = parts * CAP
    hsize = width // HEADS
    rings = parts // PLANE
    layer = rings * CORES
    y, inner = lax.div(me, layer), lax.rem(me, layer)
    z, core = lax.div(inner, CORES), lax.rem(inner, CORES)
    spot = y * CORES + core
    offsets = []
    for by in range(PLANE):
        there = lax.rem(spot + by, PLANE)
        offsets.append(lax.div(there, CORES) * layer + lax.rem(there, CORES))

    held = (
        table,
        nbr,
        own,
        row,
        feat,
        lab,
        w_query,
        w_keyval,
        w_out,
        w_msg_mem,
        w_msg_edge,
        w_pair_edge,
        gru_input,
        gru_hidden,
        gru_bias,
        bn_gain,
        bn_shift,
        w_score,
    )
    given = (
        table_h,
        nbr_h,
        own_h,
        row_h,
        feat_h,
        lab_h,
        w_query_h,
        w_keyval_h,
        w_out_h,
        w_msg_mem_h,
        w_msg_edge_h,
        w_pair_edge_h,
        gru_input_h,
        gru_hidden_h,
        gru_bias_h,
        bn_gain_h,
        bn_shift_h,
        w_score_h,
    )
    loads = [
        pltpu.make_async_copy(src, dst, load_sem.at[k])
        for k, (src, dst) in enumerate(zip(given, held))
    ]
    for k in LOAD_ORDER[:2]:
        loads[k].start()

    barrier = pltpu.get_barrier_semaphore()

    def each_turn(visit, first, last):
        if first == 0:
            visit(0)
        top = min(last, rings - 1)

        def one(turn, carry):
            visit(turn)
            return carry

        lax.fori_loop(max(first, 1), top, one, 0)
        if last == rings:
            visit(rings - 1)

    def each_peer(turn):
        base = lax.rem(z + along(turn, rings), rings) * CORES
        own_turn = isinstance(turn, int) and turn == rings - 1
        return [(by, base + offsets[by]) for by in range(1 if own_turn else 0, PLANE)]

    def greet(turn):
        for _, peer in each_peer(turn):
            pl.semaphore_signal(barrier, inc=1, device_id={"dom": peer}, device_id_type=MESH)

    each_turn(greet, NEAR, rings)
    pl.semaphore_signal(barrier, inc=1, device_id={"epoch": ahead}, device_id_type=MESH)
    for k in LOAD_ORDER[2:]:
        loads[k].start()

    def remote(src, dst, sent, received, peer):
        return pltpu.make_async_remote_copy(
            src_ref=src,
            dst_ref=dst,
            send_sem=sent,
            recv_sem=received,
            device_id={"dom": peer},
            device_id_type=MESH,
        )

    def send_turns(src, dst, which, first, last):
        def visit(turn):
            back = facing(turn, rings)
            for by, peer in each_peer(turn):
                remote(
                    src.at[turn * PLANE + by],
                    dst.at[back * PLANE + (PLANE - by) % PLANE],
                    send_sem.at[which],
                    recv_sem.at[which, lax.div(back, TURNS)],
                    peer,
                ).start()

        each_turn(visit, first, last)
        if last == rings:
            here = (rings - 1) * PLANE
            pltpu.make_async_copy(
                src.at[here], dst.at[here], recv_sem.at[which, GROUPS - 1]
            ).start()

    def send_groups(src, dst, which, first, last):
        send_turns(src, dst, which, first * TURNS, last * TURNS)

    def wait_group(dst, which, g):
        block = dst.at[pl.ds(g * TURNS * PLANE, TURNS * PLANE)]
        pltpu.make_async_copy(block, block, recv_sem.at[which, g]).wait()

    def wait_sent(dst, which):
        sent = dst.at[pl.ds(0, parts - 1)]
        pltpu.make_async_copy(sent, sent, send_sem.at[which]).wait()

    loads[2].wait()
    loads[3].wait()
    ends = 2 * events
    o = jnp.concatenate([own[0:1, :], own[1:2, :]], axis=1)
    r = jnp.concatenate([row[0:1, :], row[1:2, :]], axis=1) + 1
    away = (o // CORES - z + parts) % rings
    away = jnp.where(away == 0, rings // 2, away - rings // 2)
    turn_of = jnp.where(away > 0, 2 * away - 1, -2 * away)
    o = turn_of * PLANE + (o // layer * CORES + o % CORES - spot + PLANE) % PLANE
    owned = iota((parts, ends), 0) == o
    owned_b = onehot(owned)
    earlier = onehot(iota((ends, ends), 0) < iota((ends, ends), 1))
    before = dot(owned_b, earlier)
    rank = jnp.sum(jnp.where(owned, before, 0.0), axis=0, keepdims=True)
    rank_i = rank.astype(jnp.int32)
    ranked = iota((LANES, ends), 0) == rank_i
    high = jnp.where(ranked, (r // 32).astype(F32), 0.0).astype(BF16)
    low = jnp.where(ranked, (r % 32).astype(F32), 0.0).astype(BF16)
    asked = dot_nt(owned_b, high) * 32.0 + dot_nt(owned_b, low)
    req_s[...] = asked.reshape(parts, 1, LANES)

    pl.semaphore_wait(barrier, (rings - NEAR) * PLANE)
    for turn in range(NEAR):
        blocks = pl.ds(turn * PLANE, PLANE)
        peer = lax.rem(z + halfway(turn, rings), rings) * CORES + offsets[0]
        remote(req_s.at[blocks], relay.at[blocks], relay_send, relay_recv, peer).start()
    send_turns(req_s, req_r, 0, NEAR, rings)

    place = o * CAP + rank_i
    place_s[...] = onehot(iota((slots, ends), 0) == place)
    diagonal = iota((ends, ends), 0) == iota((ends, ends), 1)
    place_col = jnp.sum(jnp.where(diagonal, place.astype(F32), 0.0), axis=1, keepdims=True)
    place_t[...] = onehot(iota((ends, slots), 1) == place_col.astype(jnp.int32))

    for k in (0, 1, 6, 7, 8):
        loads[k].wait()
    keyval[...] = dot(table[...], w_keyval[...]).astype(BF16)
    query[...] = dot(table[...], w_query[...]).astype(BF16)

    block = LANES
    scale = 1.0 / jnp.sqrt(jnp.float32(hsize))
    for b in range(0, 2):
        here = pl.ds(b * block, block)
        times = jnp.zeros((nodes, block), F32)
        for j in range(nbr.shape[0]):
            times = times + jnp.where(iota((nodes, block), 0) == nbr[j : j + 1, here], 1.0, 0.0)
        for h in range(HEADS):
            cols = pl.ds(h * hsize, hsize)
            score = dot_nt(keyval[:, cols], query[here, cols]) * scale
            score = jnp.where(times > 0, score, -1e30)
            top = jnp.max(score, axis=0, keepdims=True)
            grown = jnp.exp(score - top)
            total = jnp.sum(grown * times, axis=0, keepdims=True)
            weight = (grown / total).astype(BF16).astype(F32) * times
            main = weight.astype(BF16)
            rest = (weight - main.astype(F32)).astype(BF16)
            value = keyval[:, pl.ds(width + h * hsize, hsize)]
            attended[here, cols] = (dot_tn(main, value) + dot_tn(rest, value)).astype(BF16)
    pltpu.make_async_copy(relay, relay, relay_recv).wait()
    for turn in range(NEAR):
        onward = along(turn, rings) - halfway(turn, rings) + rings
        base = lax.rem(z + onward, rings) * CORES
        back = facing(turn, rings)
        for by in range(PLANE):
            remote(
                relay.at[turn * PLANE + by],
                req_r.at[back * PLANE + (PLANE - by) % PLANE],
                send_sem.at[0],
                recv_sem.at[0, back // TURNS],
                base + offsets[by],
            ).start()

    gslots = slots // GROUPS
    gblocks = parts // GROUPS
    mine = iota((gblocks, CAP, LANES), 1) == iota((gblocks, CAP, LANES), 2)
    asked_for = {}
    for g in ORDER_M:
        here, blocks = pl.ds(g * gslots, gslots), pl.ds(g * gblocks, gblocks)
        wait_group(req_r, 0, g)
        got = jnp.broadcast_to(req_r[blocks], (gblocks, CAP, LANES))
        wanted = jnp.sum(jnp.where(mine, got, 0.0), axis=2, keepdims=True).reshape(gslots, 1)
        asked_for[g] = wanted
        pick[here, :] = onehot(iota((gslots, nodes), 1) + 1 == wanted.astype(jnp.int32))
        mem_s[blocks] = pack(dot(pick[here, :], table[...]))
        send_groups(mem_s, mem_r, 1, g, g + 1)
    for b in range(2, nodes // block):
        here = pl.ds(b * block, block)
        times = jnp.zeros((nodes, block), F32)
        for j in range(nbr.shape[0]):
            times = times + jnp.where(iota((nodes, block), 0) == nbr[j : j + 1, here], 1.0, 0.0)
        for h in range(HEADS):
            cols = pl.ds(h * hsize, hsize)
            score = dot_nt(keyval[:, cols], query[here, cols]) * scale
            score = jnp.where(times > 0, score, -1e30)
            top = jnp.max(score, axis=0, keepdims=True)
            grown = jnp.exp(score - top)
            total = jnp.sum(grown * times, axis=0, keepdims=True)
            weight = (grown / total).astype(BF16).astype(F32) * times
            main = weight.astype(BF16)
            rest = (weight - main.astype(F32)).astype(BF16)
            value = keyval[:, pl.ds(width + h * hsize, hsize)]
            attended[here, cols] = (dot_tn(main, value) + dot_tn(rest, value)).astype(BF16)
    embed[...] = (table[...].astype(F32) + dot(attended[...], w_out[...])).astype(BF16)

    for g in ORDER_E:
        here, blocks = pl.ds(g * gslots, gslots), pl.ds(g * gblocks, gblocks)
        emb_s[blocks] = pack(dot(pick[here, :], embed[...]))
        send_groups(emb_s, emb_r, 2, g, g + 1)

    for k in (4, 5, 9, 10, 11, 12, 13, 14, 15, 16, 17):
        loads[k].wait()
    wanted = jnp.concatenate([asked_for[g] for g in range(GROUPS)], axis=0)
    square = iota((slots, slots), 0) == iota((slots, slots), 1)
    wanted_row = jnp.sum(jnp.where(square, wanted, 0.0), axis=0, keepdims=True)
    pick_t[...] = onehot(iota((nodes, slots), 0) + 1 == wanted_row.astype(jnp.int32))
    times_named[...] = dot(pick_t[...], jnp.ones((slots, LANES), BF16))
    hidden[...] = dot(table[...], gru_hidden[...])
    msg_edge = dot(feat[...], w_msg_edge[...])
    pair_edge = dot(feat[...], w_pair_edge[...])

    rows_back = jnp.zeros((ends, width), F32)
    for g in range(GROUPS):
        wait_group(mem_r, 1, g)
        blocks = pl.ds(g * gblocks, gblocks)
        rows_back = rows_back + dot(
            place_t[:, pl.ds(g * gslots, gslots)], unpack(mem_r[blocks])
        )
    rows_back = rows_back.astype(BF16)
    to_src = dot(rows_back[events:], w_msg_mem[...]) + msg_edge
    to_dst = dot(rows_back[:events], w_msg_mem[...]) + msg_edge
    message = jnp.concatenate([to_src, to_dst], axis=0).astype(BF16)
    for g in range(GROUPS):
        blocks = pl.ds(g * gblocks, gblocks)
        msg_s[blocks] = pack(dot(place_s[pl.ds(g * gslots, gslots), :], message))
        if g < EARLY:
            send_groups(msg_s, msg_r, 3, g, g + 1)

    ends_back = jnp.zeros((ends, width), F32)
    for g in range(GROUPS):
        wait_group(emb_r, 2, g)
        blocks = pl.ds(g * gblocks, gblocks)
        ends_back = ends_back + dot(
            place_t[:, pl.ds(g * gslots, gslots)], unpack(emb_r[blocks])
        )
    pair = ends_back[:events] * ends_back[events:] + pair_edge
    sum_one = jnp.sum(pair, axis=0, keepdims=True)
    sum_two = jnp.sum(pair * pair, axis=0, keepdims=True)
    st_r[pl.ds(spot, 1)] = jnp.concatenate([sum_one, sum_two], axis=1).reshape(1, 1, 2 * width)
    copies = []
    for by in range(1, PLANE):
        copies.append(
            remote(
                st_r.at[spot],
                st_r.at[spot],
                st_send.at[by - 1],
                st_recv.at[PLANE - 1 - by],
                z * CORES + offsets[by],
            )
        )
    for copy in copies:
        copy.start()
    for by in range(1, PLANE):
        other = lax.rem(spot + by, PLANE)
        remote(
            st_r.at[other], st_r.at[other], st_send.at[by - 1], st_recv.at[by - 1], me
        ).wait_recv()
    plane_sum = st_r[0:1] + st_r[1:2] + st_r[2:3] + st_r[3:4]
    tot_r[pl.ds(z, 1)] = plane_sum

    def spread_sums(step, carry):
        peer = lax.rem(z + step, rings) * CORES + offsets[0]
        remote(tot_r.at[z], tot_r.at[z], send_sem.at[4], tot_sem, peer).start()
        return carry

    lax.fori_loop(1, rings, spread_sums, 0)
    if EARLY < GROUPS:
        send_groups(msg_s, msg_r, 3, EARLY, GROUPS)

    chunk = nodes // NODE_CHUNKS
    for g in range(GROUPS - 1):
        wait_group(msg_r, 3, g)
        blocks = pl.ds(g * gblocks, gblocks)
        part = dot(pick_t[:, pl.ds(g * gslots, gslots)], unpack(msg_r[blocks]))
        agg[...] = part if g == 0 else agg[...] + part
    wait_group(msg_r, 3, GROUPS - 1)
    inbox = unpack(msg_r[pl.ds(parts - gblocks, gblocks)])
    hands = []
    for c in range(NODE_CHUNKS):
        here = pl.ds(c * chunk, chunk)
        count = jnp.concatenate([times_named[here, :], times_named[here, :]], axis=1)
        total = agg[here, :] + dot(pick_t[here, pl.ds(slots - gslots, gslots)], inbox)
        avg = (total / jnp.maximum(count, 1.0)).astype(BF16)
        inp = dot(avg, gru_input[...]) + gru_bias[...].reshape(1, 3 * width)
        hid = hidden[here, :]
        reset = jax.nn.sigmoid(inp[:, :width] + hid[:, :width])
        update = jax.nn.sigmoid(inp[:, width : 2 * width] + hid[:, width : 2 * width])
        cand = jnp.tanh(inp[:, 2 * width :] + reset * hid[:, 2 * width :])
        fresh = (1.0 - update) * cand + update * table[here, :].astype(F32)
        hand_s[here, :] = jnp.where(count > 0, fresh, UNTOUCHED).astype(BF16)
        hand = pltpu.make_async_remote_copy(
            src_ref=hand_s.at[here],
            dst_ref=hand_r.at[here],
            send_sem=hand_send.at[c],
            recv_sem=hand_recv.at[c],
            device_id={"epoch": after},
            device_id_type=MESH,
        )
        hand.start()
        hands.append(hand)

    others = tot_r.at[pl.ds(0, rings - 1)]
    pltpu.make_async_copy(others, others, tot_sem).wait()
    sums = tot_r[0]
    for k in range(1, rings):
        sums = sums + tot_r[k]
    count_all = jnp.float32(events * parts)
    mean = sums[:, :width] / count_all
    var = sums[:, width:] / count_all - mean * mean
    normed = (pair - mean) * lax.rsqrt(var + 1e-05) * bn_gain[...] + bn_shift[...]
    weighed = jnp.maximum(normed, 0.0) * w_score[...].astype(F32).reshape(1, width)
    logit_col = jnp.sum(weighed, axis=1, keepdims=True)
    corner = iota((events, events), 0) == iota((events, events), 1)
    logit = jnp.sum(jnp.where(corner, logit_col, 0.0), axis=0, keepdims=True)
    soft = jnp.maximum(logit, 0.0) + jnp.log1p(jnp.exp(-jnp.abs(logit)))
    terms = soft - lab[...].astype(F32) * logit
    part = jnp.sum(terms, axis=1, keepdims=True)
    ls_r[pl.ds(me, 1)] = jnp.broadcast_to(part, (1, LANES)).reshape(1, 1, LANES)

    def spread_loss(turn):
        for _, peer in each_peer(turn):
            remote(ls_r.at[me], ls_r.at[me], send_sem.at[5], ls_sem, peer).start()

    each_turn(spread_loss, 0, rings)

    for c in range(NODE_CHUNKS):
        here = pl.ds(c * chunk, chunk)
        hands[c].wait()
        handed = hand_r[here, :].astype(F32)
        fresh = hand_s[here, :].astype(F32)
        old = table[here, :].astype(F32)
        prior = jnp.where(jnp.logical_and(handed < UNTOUCHED / 2, group > 0), handed, old)
        out[here, :] = jnp.where(fresh < UNTOUCHED / 2, fresh, prior).astype(BF16)

    others = ls_r.at[pl.ds(0, parts - 1)]
    pltpu.make_async_copy(others, others, ls_sem).wait()
    loss[...] = jnp.sum(ls_r[...], axis=0) / count_all

    wait_sent(req_s, 0)
    pltpu.make_async_copy(relay, relay, relay_send).wait()
    wait_sent(mem_s, 1)
    wait_sent(emb_s, 2)
    wait_sent(msg_s, 3)
    for copy in copies:
        copy.wait_send()
    others = tot_r.at[pl.ds(0, rings - 1)]
    pltpu.make_async_copy(others, others, send_sem.at[4]).wait()
    wait_sent(ls_r, 5)


def shards(
    parts,
    groups,
    memory,
    neighbours,
    owners,
    rows,
    edge_feat,
    labels,
    w_query,
    w_keyval,
    w_out,
    w_msg_mem,
    w_msg_edge,
    w_pair_edge,
    gru_input,
    gru_hidden,
    gru_bias,
    bn_gain,
    bn_shift,
    w_score,
):
    nodes, width = memory.shape[1:]
    events = owners.shape[1]
    slots = parts * CAP
    ends = 2 * events
    block = (parts, 2 * CAP, LANES)
    line = (parts, 1, LANES)
    operands = (
        memory[0],
        neighbours.T,
        owners[0].T,
        rows[0].T,
        edge_feat[0],
        labels,
        w_query,
        w_keyval,
        w_out,
        w_msg_mem,
        w_msg_edge,
        w_pair_edge,
        gru_input,
        gru_hidden,
        gru_bias,
        bn_gain[None],
        bn_shift[None],
        w_score,
    )
    result, loss = pl.pallas_call(
        functools.partial(kernel, parts, groups),
        out_shape=(
            pltpu.VMEM((nodes, width), BF16),
            pltpu.VMEM((1, LANES), F32),
        ),
        in_specs=[pl.BlockSpec(memory_space=pl.ANY)] * 18,
        out_specs=(pl.BlockSpec(memory_space=pltpu.VMEM),) * 2,
        scratch_shapes=[
            pltpu.VMEM(line, F32),
            pltpu.VMEM(line, F32),
            pltpu.VMEM(block, BF16),
            pltpu.VMEM(block, BF16),
            pltpu.VMEM(block, BF16),
            pltpu.VMEM(block, BF16),
            pltpu.VMEM(block, BF16),
            pltpu.VMEM(block, BF16),
            pltpu.VMEM((PLANE, 1, 2 * width), F32),
            pltpu.VMEM((parts // PLANE, 1, 2 * width), F32),
            pltpu.VMEM(line, F32),
            pltpu.VMEM((nodes, width), BF16),
            pltpu.VMEM((nodes, width), BF16),
            pltpu.VMEM((nodes, 2 * width), BF16),
            pltpu.VMEM((nodes, width), BF16),
            pltpu.VMEM((nodes, width), BF16),
            pltpu.VMEM((nodes, width), BF16),
            pltpu.VMEM((nodes, 3 * width), F32),
            pltpu.VMEM((slots, nodes), BF16),
            pltpu.VMEM((nodes, slots), BF16),
            pltpu.VMEM((slots, ends), BF16),
            pltpu.VMEM((ends, slots), BF16),
            pltpu.VMEM((nodes, LANES), F32),
            pltpu.VMEM((nodes, width), F32),
            pltpu.SemaphoreType.DMA((6,)),
            pltpu.SemaphoreType.DMA((4, GROUPS)),
            pltpu.VMEM((NEAR * PLANE, 1, LANES), F32),
            pltpu.SemaphoreType.DMA,
            pltpu.SemaphoreType.DMA,
            pltpu.SemaphoreType.DMA,
            pltpu.SemaphoreType.DMA,
            pltpu.SemaphoreType.DMA((PLANE - 1,)),
            pltpu.SemaphoreType.DMA((PLANE - 1,)),
            pltpu.SemaphoreType.DMA((NODE_CHUNKS,)),
            pltpu.SemaphoreType.DMA((NODE_CHUNKS,)),
            pltpu.SemaphoreType.DMA((len(operands),)),
        ]
        + [pltpu.VMEM(x.shape, x.dtype) for x in operands],
        compiler_params=pltpu.CompilerParams(
            collective_id=0, has_side_effects=True, vmem_limit_bytes=VMEM_LIMIT
        ),
        name="window",
    )(*operands)
    return result[None], loss[0, :1]


def solution(mesh):
    parts, groups = mesh.shape["dom"], mesh.shape["epoch"]
    return jax.shard_map(
        functools.partial(shards, parts, groups),
        mesh=mesh,
        in_specs=(
            P("epoch", "dom", None),
            P("dom", None),
            P("epoch", "dom", None),
            P("epoch", "dom", None),
            P("epoch", "dom", None),
            P("epoch", "dom"),
            P(),
            P(),
            P(),
            P(),
            P(),
            P(),
            P(),
            P(),
            P(),
            P(),
            P(),
            P(),
        ),
        out_specs=(P("epoch", "dom", None), P("epoch")),
        check_vma=False,
    )
```
